32 devices in a mesh: rep: 2 (over y), fsdp: 16 (over z, x, core).
Axes of the slice: x: 2, y: 2, z: 4, core: 2. Of those that a mesh axis runs over, the one named last changes fastest.
Arguments:
- hidden: bfloat16 [8192, 5120], P(('rep', 'fsdp')), may hold values from -6 to 6
- weight: bfloat16 [640, 64, 128], P('fsdp'), may hold values from -0.078125 to 0.078125
- momentum: float32 [2, 640, 64, 128], P('rep', 'fsdp'), may hold values from -6 to 6
- gradient: bfloat16 [2, 640, 64, 128], P('rep', 'fsdp'), may hold values from -6 to 6
- indices: int32 [2, 1280, 32], P('rep', 'fsdp'), may hold values from 0 to 4095, as said below
- counts: int32 [2, 1280], P('rep', 'fsdp'), may hold values from 1 to 32, as said below
Outputs:
- key_states: bfloat16 [8192, 1024], P(('rep', 'fsdp'))
- update: bfloat16 [640, 64, 128], P('fsdp', 'rep')
- new_momentum: float32 [2, 640, 64, 128], P('rep', 'fsdp')
The draws below stay inside these ranges and needn't reach their ends.
Inputs may be any that keep to these rules, and one draw needn't show every extreme that they name: `indices`: the 32 numbers of one replica's block differ from one another. `counts`: some block of every replica keeps all 32.
All inputs are finite; a program needn't handle non-finite values.
Results may differ from the reference program's by a relative error of at most 0.0095.
Values may be sent and summed in bfloat16 or wider, within the bound.
A program may use at most 128 MiB of HBM per device.

```python
import jax
import jax.numpy as jnp
from jax import lax

D = 5120
KV = 1024
CH = 64
TOPK = 32
TOK_DEV = 256
TILES = 640
SPANS = 1280
TOKEN_TOTAL = 8192
N_REP = 2


def draw_indices(key, part):
    key = jax.random.fold_in(key, 11)
    replica_keys = jax.random.split(key, N_REP)

    def one_replica(sub_key):
        scores = jax.random.randint(sub_key, (SPANS, CH * CH), 0, 2 ** 18)
        scores = scores * (CH * CH) + jnp.arange(CH * CH, dtype=jnp.int32)[None, :]
        return lax.top_k(scores, TOPK)[1].astype(jnp.int32)
    return lax.map(one_replica, replica_keys)


def draw_counts(key, part):
    key = jax.random.fold_in(key, 23)
    first_key, second_key = jax.random.split(key)
    drawn = jax.random.randint(first_key, (N_REP, SPANS), 1, TOPK + 1)
    complete_block = jax.random.randint(second_key, (N_REP, 1), 0, SPANS)
    position = jnp.arange(SPANS, dtype=jnp.int32)[None, :]
    return jnp.where(position == complete_block, TOPK, drawn).astype(jnp.int32)


def levels(rng, dims, cuts, least, largest):
    factor_of = 1.0
    for dim, blocks in cuts:
        steps = jax.random.uniform(jax.random.fold_in(jax.random.fold_in(rng, 6), dim), (blocks,), jnp.float32, least / len(cuts), largest / len(cuts))
        factor_of = factor_of * jnp.repeat(jnp.exp(steps), dims[dim] // blocks).reshape((-1,) + (1,) * (len(dims) - 1 - dim))
    return factor_of


def gaussian(own_key, shape, scale, most, cuts=(), kind=jnp.bfloat16):
    loudness = levels(own_key, shape, cuts, -0.22, 0.18) if cuts else 1.0
    values = jax.random.normal(own_key, shape, jnp.float32) * scale * loudness
    return jnp.minimum(jnp.maximum(values, -most), most).astype(kind)


def setup_inputs(seed: int = 0) -> dict:
    arg_keys = jax.random.split(jax.random.key(seed), 7)
    hidden = gaussian(arg_keys[0], (TOKEN_TOTAL, D), 1.0, 6.0, ((0, 32),))
    weight = gaussian(arg_keys[1], (TILES, CH, 2 * CH), D ** -0.5, 0.078125, ((0, 16),))
    momentum = gaussian(arg_keys[2], (N_REP, TILES, CH, 2 * CH), 1.0, 6.0, ((0, 2), (1, 16)), jnp.float32)
    gradient = gaussian(arg_keys[3], (N_REP, TILES, CH, 2 * CH), 1.0, 6.0, ((0, 2), (1, 16)))
    indices = draw_indices(jax.random.fold_in(arg_keys[6], 71), 0)
    counts = draw_counts(jax.random.fold_in(arg_keys[6], 71), 0)
    return dict(hidden=hidden, weight=weight, momentum=momentum, gradient=gradient, indices=indices, counts=counts)


decay_rate = 0.999
step_size = 0.01
tiny_eps = 1e-06

def dct_table(length):
    wave_number = jnp.arange(length, dtype=jnp.float32)[:, None]
    position = jnp.arange(length, dtype=jnp.float32)[None, :]
    dct_rows = jnp.cos(jnp.pi * (2.0 * position + 1.0) * wave_number / (2.0 * length)) * jnp.sqrt(2.0 / length)
    return jnp.where(wave_number == 0.0, dct_rows * jnp.sqrt(0.5), dct_rows)

def to_spectrum(blocks, dct_rows):
    return jnp.einsum('ka,...ab,lb->...kl', dct_rows, blocks, dct_rows, precision=lax.Precision.HIGHEST)

def from_spectrum(tile_frequency_coefficients, dct_rows):
    return jnp.einsum('ka,...kl,lb->...ab', dct_rows, tile_frequency_coefficients, dct_rows, precision=lax.Precision.HIGHEST)

def reference(hidden, weight, momentum, gradient, indices, counts):
    dct_rows = dct_table(CH)
    moment = decay_rate * momentum + gradient.astype(jnp.float32)
    blocks = moment.reshape(N_REP, TILES, CH, 2, CH).transpose(0, 1, 3, 2, 4).reshape(N_REP, SPANS, CH, CH)
    tile_frequency_coefficients = to_spectrum(blocks, dct_rows).reshape(N_REP, SPANS, CH * CH)
    picked = jnp.take_along_axis(tile_frequency_coefficients, indices, axis=2)
    is_live = jnp.arange(TOPK, dtype=jnp.int32)[None, None, :] < counts[:, :, None]
    kept_values = jnp.where(is_live, picked, jnp.zeros_like(picked))
    replica_rows = jnp.arange(N_REP, dtype=jnp.int32)[:, None, None]
    span_rows = jnp.arange(SPANS, dtype=jnp.int32)[None, :, None]
    own_spectra = jnp.zeros((N_REP, SPANS, CH * CH), jnp.float32).at[replica_rows, span_rows, indices].add(kept_values)
    own_spectra = own_spectra.reshape(N_REP, SPANS, CH, CH)
    estimate = from_spectrum(own_spectra, dct_rows)
    new_blocks = blocks - estimate
    new_momentum = new_blocks.reshape(N_REP, TILES, 2, CH, CH).transpose(0, 1, 3, 2, 4).reshape(N_REP, TILES, CH, 2 * CH)
    shared = lax.optimization_barrier(jnp.sum(own_spectra, axis=0)) / N_REP
    raw_descent_direction = from_spectrum(shared, dct_rows)
    span_scale = jnp.sqrt(lax.optimization_barrier(jnp.mean(raw_descent_direction * raw_descent_direction, axis=(1, 2), keepdims=True)) + tiny_eps)
    update = jnp.tanh(raw_descent_direction / span_scale).astype(jnp.bfloat16)
    update = update.reshape(TILES, 2, CH, CH).transpose(0, 2, 1, 3).reshape(TILES, CH, 2 * CH)
    revised_parameters = (weight.astype(jnp.float32) - step_size * update.astype(jnp.float32)).astype(jnp.bfloat16)
    matrix = revised_parameters.reshape(KV // (2 * CH), D // CH, CH, 2 * CH).transpose(1, 2, 0, 3).reshape(D, KV)

    def project(row_block):
        return jnp.dot(row_block, matrix, preferred_element_type=jnp.float32).astype(jnp.bfloat16)
    key_states = lax.map(project, hidden.reshape(TOKEN_TOTAL // TOK_DEV, TOK_DEV, D)).reshape(TOKEN_TOTAL, KV)
    return (key_states, update, new_momentum)
```

```python
import functools

import jax
import jax.numpy as jnp
import numpy as np
from jax import lax
from jax.experimental import pallas as pl
from jax.experimental.pallas import tpu as pltpu
from jax.sharding import PartitionSpec as P

decay_rate = 0.999
step_size = 0.01
tiny_eps = 1e-06
exact = lax.Precision.HIGHEST
MESH = pl.DeviceIdType.MESH
CHUNKS = 5


def cosine_table(length):
    wave = np.arange(length, dtype=np.float64)[:, None]
    place = np.arange(length, dtype=np.float64)[None, :]
    table = np.cos(np.pi * (2.0 * place + 1.0) * wave / (2.0 * length)) * np.sqrt(2.0 / length)
    return np.where(wave == 0.0, table * np.sqrt(0.5), table)


def split(value):
    high = value.astype(jnp.bfloat16)
    return high, (value - high.astype(jnp.float32)).astype(jnp.bfloat16)


def dot(a, b):
    return jnp.dot(a, b, preferred_element_type=jnp.float32)


def dot_nt(a, b):
    return lax.dot_general(a, b, (((1,), (1,)), ((), ())), preferred_element_type=jnp.float32)


def right3(a, b_high, b_low):
    high, low = split(a)
    return dot(high, b_high) + (dot(high, b_low) + dot(low, b_high))


def left3(a_high, a_low, b):
    high, low = split(b)
    return dot(a_high, high) + (dot(a_high, low) + dot(a_low, high))


def fused_kernel(
    hidden,
    weight,
    momentum,
    gradient,
    index,
    basis,
    basis_high,
    basis_low,
    keys,
    update,
    new_momentum,
    blocks,
    tokens,
    total,
    partial,
    spectra,
    kept,
    kept_other,
    index_other,
    recv_sem,
    z_sem,
    x_sem,
    y_sem,
    small_send,
    small_recv,
    part_send,
    part_recv,
):
    tiles, side, cols = weight.shape
    per = tiles // CHUNKS
    rows = per * side
    half = tiles * side
    own_tokens = hidden.shape[0]
    pair = 2 * side
    four = 4 * side

    r = lax.axis_index("rep")
    f = lax.axis_index("fsdp")
    z, x, c = f // 4, (f // 2) % 2, f % 2
    middle = jnp.logical_and(z > 0, z < 3)
    up_ok, down_ok = z < 3, z > 0
    y_dev = (1 - r, f)
    x_dev = (r, z * 4 + (1 - x) * 2 + c)
    sib_dev = (r, z * 4 + x * 2 + (1 - c))
    up_dev = (r, jnp.minimum(f + 4, 15 - 3 + f % 4))
    down_dev = (r, jnp.maximum(f - 4, f % 4))

    barrier = pltpu.get_barrier_semaphore()
    for device in (y_dev, x_dev, sib_dev):
        pl.semaphore_signal(barrier, inc=1, device_id=device, device_id_type=MESH)

    @pl.when(up_ok)
    def _():
        pl.semaphore_signal(barrier, inc=1, device_id=up_dev, device_id_type=MESH)

    @pl.when(down_ok)
    def _():
        pl.semaphore_signal(barrier, inc=1, device_id=down_dev, device_id_type=MESH)

    pl.semaphore_wait(barrier, jnp.where(middle, 5, 4))

    def remote(src, dst, send, recv, device):
        return pltpu.make_async_remote_copy(
            src_ref=src, dst_ref=dst, send_sem=send, recv_sem=recv, device_id=device, device_id_type=MESH
        )

    index_copy = remote(index, index_other, small_send.at[0], small_recv.at[0], y_dev)
    index_copy.start()
    token_copy = remote(
        hidden.at[:, pl.ds(pl.multiple_of((1 - c) * half, 128), half)],
        tokens.at[pl.ds(own_tokens, own_tokens)],
        small_send.at[1],
        small_recv.at[1],
        sib_dev,
    )
    token_copy.start()
    token_local = pltpu.make_async_copy(
        hidden.at[:, pl.ds(pl.multiple_of(c * half, 128), half)],
        tokens.at[pl.ds(0, own_tokens)],
        small_send.at[3],
    )
    token_local.start()

    def place(p):
        return jnp.where(r == 0, p, CHUNKS - 1 - p)

    def layer(j):
        if j == 0:
            return z
        at_end = jnp.where(z == 0, j, 3 - j)
        flip = (1, 3, 2)[j - 1]
        bits = z // 2, z % 2
        inner = ((bits[0] + flip // 2) % 2) * 2 + (bits[1] + flip % 2) % 2
        return jnp.where(middle, inner, at_end)

    def chunk(o, p):
        q = place(p)
        ref = blocks.at[o, pl.ds(pl.multiple_of(q * rows, rows), rows)]
        return ref, o * CHUNKS + q

    def move(o, p, sems, device):
        ref, n = chunk(o, p)
        return remote(ref, ref, sems.at[n], recv_sem.at[n], device)

    def z_move(o, p, way):
        return move(o, p, z_sem.at[way], up_dev if way == 0 else down_dev)

    lane = lax.broadcasted_iota(jnp.int32, (1, cols), 1)
    row_iota = lax.broadcasted_iota(jnp.int32, (side, cols), 0)
    col_iota = lax.broadcasted_iota(jnp.int32, (cols, cols), 0)
    left_lanes = lane < side
    second = jnp.where(lane % side >= side // 2, side, 0)

    def hot_rows(idx):
        return row_iota == (idx >> 6)

    def hot_cols(idx):
        return (col_iota == ((idx & (side - 1)) + second)).astype(jnp.bfloat16)

    def both_halves(value):
        return jnp.concatenate([value[:four], value[four:]], axis=1)

    def stacked(value):
        return jnp.concatenate([value[:, :cols], value[:, cols:]], axis=0)

    def inverse(coefficients):
        part = right3(coefficients, basis_high[0, :pair, :pair], basis_low[0, :pair, :pair])
        return stacked(left3(basis_high[1], basis_low[1], both_halves(part)))

    def tile_slice(q):
        return pl.ds(pl.multiple_of(q * per, per), per)

    def forward(q, carry):
        here = tile_slice(q)
        moment = decay_rate * momentum[0, here] + gradient[0, here].astype(jnp.float32)
        new_momentum[0, here] = moment
        part = jnp.dot(
            moment.reshape(rows, cols),
            basis[1, :pair, :pair],
            precision=exact,
            preferred_element_type=jnp.float32,
        )
        spectrum = stacked(
            jnp.dot(basis[0], both_halves(part), precision=exact, preferred_element_type=jnp.float32)
        )
        spectra[pl.ds(pl.multiple_of(q * rows, rows), rows)] = spectrum
        idx = index[here]
        found = []
        for t in range(per):
            one = idx[t : t + 1]
            high, low = split(spectrum[t * side : (t + 1) * side])
            taken = dot(jnp.concatenate([high, low], axis=0), hot_cols(one))
            taken = taken[:side] + taken[side:]
            found.append(jnp.sum(jnp.where(hot_rows(one), taken, 0.0), axis=0, keepdims=True))
        kept[here] = jnp.concatenate(found, axis=0)
        return carry

    lax.fori_loop(0, CHUNKS, forward, 0)
    kept_copy = remote(kept, kept_other, small_send.at[2], small_recv.at[2], y_dev)
    kept_copy.start()
    index_copy.wait_recv()
    kept_copy.wait_recv()

    own_block = 2 * z + x

    def step(p, carry):
        q = place(p)
        here = tile_slice(q)
        idx = jnp.where(left_lanes, index[here], index_other[here])
        values = jnp.where(left_lanes, kept[here], kept_other[here]) * 0.5
        dense = []
        for t in range(per):
            one = idx[t : t + 1]
            high, low = split(jnp.where(hot_rows(one), values[t : t + 1], 0.0))
            put = dot_nt(jnp.concatenate([high, low], axis=0), hot_cols(one))
            tile = put[:side] + put[side:]
            energy = jnp.sum(tile * tile, axis=0, keepdims=True)
            left = jnp.sum(jnp.where(left_lanes, energy, 0.0), axis=1, keepdims=True)
            right = jnp.sum(jnp.where(left_lanes, 0.0, energy), axis=1, keepdims=True)
            energy = jnp.where(left_lanes, left, right)
            dense.append(tile * lax.rsqrt(energy / (side * side) + tiny_eps))
        raw = inverse(jnp.concatenate(dense, axis=0))
        direction = jnp.tanh(raw).astype(jnp.bfloat16).astype(jnp.float32)
        tiled = direction.reshape(per, side, cols)
        shown = jnp.where(r == 0, tiled[:, : side // 2], tiled[:, side // 2 :])
        update[here] = shown.astype(jnp.bfloat16)
        old = weight[here].astype(jnp.float32).reshape(rows, cols)
        blocks[own_block, pl.ds(pl.multiple_of(q * rows, rows), rows)] = (
            old - step_size * direction
        ).astype(jnp.bfloat16)

        @pl.when(jnp.logical_and(up_ok, p < 4))
        def _():
            z_move(own_block, p, 0).start()

        @pl.when(jnp.logical_and(down_ok, p < 4))
        def _():
            z_move(own_block, p, 1).start()

        @pl.when(p < 3)
        def _():
            move(own_block, p, x_sem, x_dev).start()

        return carry

    lax.fori_loop(0, CHUNKS, step, 0)

    def settle(q, carry):
        here = tile_slice(q)
        idx = index[here]
        spectrum = spectra[pl.ds(pl.multiple_of(q * rows, rows), rows)]
        masks = []
        for t in range(per):
            one = idx[t : t + 1]
            hot = jnp.where(jnp.logical_and(hot_rows(one), left_lanes), 1.0, 0.0).astype(jnp.bfloat16)
            masks.append(dot_nt(hot, hot_cols(one)))
        own = jnp.where(jnp.concatenate(masks, axis=0) > 0.5, spectrum, 0.0)
        new_momentum[0, here] = new_momentum[0, here] - inverse(own).reshape(per, side, cols)
        return carry

    lax.fori_loop(0, CHUNKS, settle, 0)
    token_local.wait()
    token_copy.wait_recv()

    def arrived(o, p):
        move(o, p, x_sem, x_dev).wait_recv()

    def from_z(j, p):
        o = 2 * layer(j) + x
        arrived(o, p)
        below = layer(j) < z

        @pl.when(jnp.logical_and(below, up_ok))
        def _():
            z_move(o, p, 0).start()

        @pl.when(jnp.logical_and(jnp.logical_not(below), down_ok))
        def _():
            z_move(o, p, 1).start()

        if p < 3:
            move(o, p, x_sem, x_dev).start()
        if p == 0:
            move(o, p, y_sem, y_dev).start()

    def from_x(j, p):
        o = 2 * layer(j) + (1 - x)
        arrived(o, p)
        if p < 2:
            move(o, p, y_sem, y_dev).start()

    def part_copy(j):
        return remote(
            total.at[j, pl.ds(own_tokens, own_tokens)], partial.at[j], part_send.at[j], part_recv.at[j], sib_dev
        )

    def multiply(j):
        o = 2 * layer(j)

        def product(k):
            deep = pl.ds(pl.multiple_of(k * rows, rows), rows)
            both = jnp.concatenate([blocks[o, deep], blocks[o + 1, deep]], axis=1)
            return dot(tokens[:, deep], both)

        total[j] = product(0)

        def add(k, carry):
            total[j] += product(k)
            return carry

        lax.fori_loop(1, CHUNKS, add, 0)
        part_copy(j).start()

    for j in range(5):
        for p in range(4):
            if 1 <= j + 1 <= 3:
                from_z(j + 1, p)
            if j < 4 and p < 3:
                from_x(j, p)
        if j < 4:
            if j > 0:
                arrived(2 * layer(j) + x, 4)
            arrived(2 * layer(j) + (1 - x), 4)
            arrived(2 * layer(j) + (1 - x), 3)
            multiply(j)

    for j in range(4):
        part_copy(j).wait_recv()
        columns = pl.ds(pl.multiple_of(layer(j) * 2 * cols, 2 * cols), 2 * cols)
        keys[:, columns] = (total[j, :own_tokens] + partial[j]).astype(jnp.bfloat16)

    index_copy.wait_send()
    token_copy.wait_send()
    kept_copy.wait_send()
    for j in range(4):
        part_copy(j).wait_send()
        o = 2 * layer(j) + x
        below = layer(j) < z
        above = layer(j) > z
        goes_up = jnp.logical_and(jnp.logical_not(above), up_ok)
        goes_down = jnp.logical_and(jnp.logical_not(below), down_ok)
        for p in range(4):

            @pl.when(goes_up)
            def _():
                z_move(o, p, 0).wait_send()

            @pl.when(goes_down)
            def _():
                z_move(o, p, 1).wait_send()

            if p < 3:
                move(o, p, x_sem, x_dev).wait_send()
        if j > 0:
            move(o, 0, y_sem, y_dev).wait_send()
        for p in range(2):
            move(2 * layer(j) + (1 - x), p, y_sem, y_dev).wait_send()


def fused(hidden, weight, momentum, gradient, indices, counts):
    tiles, side, cols = weight.shape
    kept_count = indices.shape[2]
    half = tiles * side
    own_tokens = hidden.shape[0]
    live = jnp.arange(kept_count, dtype=jnp.int32)[None, :] < counts[0][:, None]
    index = jnp.where(live, indices[0], -1).reshape(tiles, 2 * kept_count)
    index = jnp.concatenate([index, index], axis=1)
    table = np.kron(np.eye(4), cosine_table(side))
    basis = np.stack([table, table.T]).astype(np.float32)
    basis_high = basis.astype(jnp.bfloat16)
    basis_low = (basis - basis_high.astype(np.float32)).astype(jnp.bfloat16)
    vmem = pl.BlockSpec(memory_space=pltpu.VMEM)
    number = 8 * CHUNKS
    dma = pltpu.SemaphoreType.DMA
    keys, update, new_momentum = pl.pallas_call(
        fused_kernel,
        out_shape=(
            jax.ShapeDtypeStruct((own_tokens, 8 * cols), jnp.bfloat16),
            jax.ShapeDtypeStruct((tiles, side // 2, cols), jnp.bfloat16),
            jax.ShapeDtypeStruct(momentum.shape, jnp.float32),
        ),
        in_specs=[pl.BlockSpec(memory_space=pl.ANY)] + [vmem] * 7,
        out_specs=(vmem, vmem, vmem),
        scratch_shapes=[
            pltpu.VMEM((8, half, cols), jnp.bfloat16),
            pltpu.VMEM((2 * own_tokens, half), jnp.bfloat16),
            pltpu.VMEM((4, 2 * own_tokens, 2 * cols), jnp.float32),
            pltpu.VMEM((4, own_tokens, 2 * cols), jnp.float32),
            pltpu.VMEM((half, cols), jnp.float32),
            pltpu.VMEM((tiles, cols), jnp.float32),
            pltpu.VMEM((tiles, cols), jnp.float32),
            pltpu.VMEM((tiles, cols), jnp.int32),
            dma((number,)),
            dma((2, number)),
            dma((number,)),
            dma((number,)),
            dma((4,)),
            dma((3,)),
            dma((4,)),
            dma((4,)),
        ],
        compiler_params=pltpu.CompilerParams(
            collective_id=0, has_side_effects=True, vmem_limit_bytes=48 * 1024 * 1024
        ),
    )(
        hidden,
        weight,
        momentum,
        gradient,
        index,
        jnp.asarray(basis),
        jnp.asarray(basis_high),
        jnp.asarray(basis_low),
    )
    return keys, update, new_momentum


finest_numeric_accuracy = lax.Precision.HIGHEST


def dct_table(length):
    wave_number = jnp.arange(length, dtype=jnp.float32)[:, None]
    position = jnp.arange(length, dtype=jnp.float32)[None, :]
    dct_rows = jnp.cos(jnp.pi * (2.0 * position + 1.0) * wave_number / (2.0 * length)) * jnp.sqrt(
        2.0 / length
    )
    return jnp.where(wave_number == 0.0, dct_rows * jnp.sqrt(0.5), dct_rows)


def make_pair(dct_rows):
    empty_square_tile = jnp.zeros_like(dct_rows)
    upper_half = jnp.concatenate([dct_rows, empty_square_tile], axis=1)
    lower_half = jnp.concatenate([empty_square_tile, dct_rows], axis=1)
    return jnp.concatenate([upper_half, lower_half], axis=0)


def to_spectrum(tile_data, row_basis_operator, paired_cosine_matrix):
    partial_transform = jnp.einsum(
        "ka,tab->tkb", row_basis_operator, tile_data, precision=finest_numeric_accuracy
    )
    return jnp.einsum(
        "tkb,cb->tkc", partial_transform, paired_cosine_matrix, precision=finest_numeric_accuracy
    )


def from_spectrum(tile_frequency_coefficients, row_basis_operator, paired_cosine_matrix):
    partial_transform = jnp.einsum(
        "yh,kyi->khi",
        row_basis_operator,
        tile_frequency_coefficients,
        precision=finest_numeric_accuracy,
    )
    return jnp.einsum(
        "pln,ns->pls", partial_transform, paired_cosine_matrix, precision=finest_numeric_accuracy
    )


def plain(hidden, weight, momentum, gradient, indices, counts):
    tiles_dev, block_side, tile_cols = weight.shape
    kept_count = indices.shape[2]
    replicas = lax.axis_size("rep")
    group_size = lax.axis_size("fsdp")
    all_tiles = tiles_dev * group_size
    width = hidden.shape[1]
    dct_rows = dct_table(block_side)
    paired_cosine_matrix = make_pair(dct_rows)
    moment = decay_rate * momentum[0] + gradient[0].astype(jnp.float32)
    tile_frequency_coefficients = to_spectrum(moment, dct_rows, paired_cosine_matrix)
    span_ids = jnp.arange(2 * tiles_dev, dtype=jnp.int32)[:, None]
    places = (
        span_ids // 2 * (block_side * tile_cols)
        + indices[0] // block_side * tile_cols
        + span_ids % 2 * block_side
        + indices[0] % block_side
    )
    picked = tile_frequency_coefficients.reshape(-1)[places]
    is_live = jnp.arange(kept_count, dtype=jnp.int32)[None, :] < counts[0][:, None]
    kept_values = jnp.where(is_live, picked, jnp.zeros_like(picked))
    flat_size = tiles_dev * block_side * tile_cols
    own_spectra = (
        jnp.zeros((flat_size,), jnp.float32).at[places.reshape(-1)].add(kept_values.reshape(-1))
    )
    own_spectra = own_spectra.reshape(tiles_dev, block_side, tile_cols)
    new_momentum = (moment - from_spectrum(own_spectra, dct_rows, paired_cosine_matrix))[None]
    all_places, all_values = (
        lax.all_gather(places[None], "rep", axis=0, tiled=True),
        lax.all_gather(kept_values[None], "rep", axis=0, tiled=True),
    )
    shared = (
        jnp.zeros((flat_size,), jnp.float32).at[all_places.reshape(-1)].add(all_values.reshape(-1))
    )
    shared = shared.reshape(tiles_dev, block_side, tile_cols) / replicas
    energy = jnp.sum((shared * shared).reshape(tiles_dev, block_side, 2, block_side), axis=(1, 3))
    span_scale = jnp.sqrt(energy / (block_side * block_side) + tiny_eps)
    span_scale = jnp.repeat(span_scale, block_side, axis=1)[:, None, :]
    rows_rep = block_side // replicas
    row_first = lax.axis_index("rep") * rows_rep
    raw_descent_direction = from_spectrum(shared, dct_rows, paired_cosine_matrix)
    update = jnp.tanh(raw_descent_direction / span_scale).astype(jnp.bfloat16)
    revised_parameters = (
        weight.astype(jnp.float32) - step_size * update.astype(jnp.float32)
    ).astype(jnp.bfloat16)
    assembled = lax.all_gather(revised_parameters, "fsdp", axis=0, tiled=True)
    out_update = lax.dynamic_slice_in_dim(update, row_first, rows_rep, 1)
    out_blocks = all_tiles // (width // block_side)
    matrix = assembled.reshape(out_blocks, width // block_side, block_side, tile_cols).transpose(
        1, 2, 0, 3
    )
    matrix = matrix.reshape(width, out_blocks * tile_cols)
    key_states = jnp.dot(hidden, matrix, preferred_element_type=jnp.float32).astype(jnp.bfloat16)
    return (key_states, out_update, new_momentum)


def solution(mesh):
    in_specs = (
        P(("rep", "fsdp"), None),
        P("fsdp", None, None),
        P("rep", "fsdp", None, None),
        P("rep", "fsdp", None, None),
        P("rep", "fsdp", None),
        P("rep", "fsdp"),
    )
    out_specs = (P(("rep", "fsdp"), None), P("fsdp", "rep", None), P("rep", "fsdp", None, None))
    small = mesh.shape["rep"] == 2 and mesh.shape["fsdp"] == 16
    shards = fused if small else plain
    return jax.shard_map(shards, mesh=mesh, in_specs=in_specs, out_specs=out_specs, check_vma=False)
```

```python
import functools

import jax
import jax.numpy as jnp
import numpy as np
from jax import lax
from jax.experimental import pallas as pl
from jax.experimental.pallas import tpu as pltpu
from jax.sharding import PartitionSpec as P

decay_rate = 0.999
step_size = 0.01
tiny_eps = 1e-06
exact = lax.Precision.HIGHEST
MESH = pl.DeviceIdType.MESH
CHUNKS = 5


def cosine_table(length):
    wave = np.arange(length, dtype=np.float64)[:, None]
    place = np.arange(length, dtype=np.float64)[None, :]
    table = np.cos(np.pi * (2.0 * place + 1.0) * wave / (2.0 * length)) * np.sqrt(2.0 / length)
    return np.where(wave == 0.0, table * np.sqrt(0.5), table)


def split(value):
    high = value.astype(jnp.bfloat16)
    return high, (value - high.astype(jnp.float32)).astype(jnp.bfloat16)


def dot(a, b):
    return jnp.dot(a, b, preferred_element_type=jnp.float32)


def dot_nt(a, b):
    return lax.dot_general(a, b, (((1,), (1,)), ((), ())), preferred_element_type=jnp.float32)


def split3(value):
    high = value.astype(jnp.bfloat16)
    rest = value - high.astype(jnp.float32)
    middle = rest.astype(jnp.bfloat16)
    return high, middle, (rest - middle.astype(jnp.float32)).astype(jnp.bfloat16)


def fused_kernel(
    hidden,
    weight_hbm,
    momentum_hbm,
    gradient_hbm,
    indices,
    counts,
    basis_hbm,
    keys,
    update,
    new_momentum,
    blocks,
    tokens,
    total,
    partial,
    spectra,
    kept,
    kept_other,
    index_other,
    index,
    weight,
    momentum,
    gradient,
    basis,
    raw_index,
    raw_count,
    spread,
    load_sem,
    recv_sem,
    z_sem,
    x_sem,
    y_sem,
    small_send,
    small_recv,
    kept_send,
    kept_recv,
    part_send,
    part_recv,
):
    loads = [
        pltpu.make_async_copy(src, dst, load_sem.at[n])
        for n, (src, dst) in enumerate(
            (
                (indices.at[0], raw_index),
                (counts, raw_count),
                (basis_hbm, basis),
                (momentum_hbm.at[0], momentum),
                (gradient_hbm.at[0], gradient),
                (weight_hbm, weight),
            )
        )
    ]
    for load in loads:
        load.start()
    tiles, side, cols = weight.shape
    per = tiles // CHUNKS
    rows = per * side
    half = tiles * side
    own_tokens = hidden.shape[0]
    pair = 2 * side
    four = 4 * side

    r = lax.axis_index("rep")
    f = lax.axis_index("fsdp")
    z, x, c = f // 4, (f // 2) % 2, f % 2
    middle = jnp.logical_and(z > 0, z < 3)
    up_ok, down_ok = z < 3, z > 0
    y_dev = (1 - r, f)
    x_dev = (r, z * 4 + (1 - x) * 2 + c)
    sib_dev = (r, z * 4 + x * 2 + (1 - c))
    up_dev = (r, jnp.minimum(f + 4, 15 - 3 + f % 4))
    down_dev = (r, jnp.maximum(f - 4, f % 4))

    barrier = pltpu.get_barrier_semaphore()
    for device in (y_dev, x_dev, sib_dev):
        pl.semaphore_signal(barrier, inc=1, device_id=device, device_id_type=MESH)

    @pl.when(up_ok)
    def _():
        pl.semaphore_signal(barrier, inc=1, device_id=up_dev, device_id_type=MESH)

    @pl.when(down_ok)
    def _():
        pl.semaphore_signal(barrier, inc=1, device_id=down_dev, device_id_type=MESH)

    pl.semaphore_wait(barrier, jnp.where(middle, 5, 4))

    def remote(src, dst, send, recv, device):
        return pltpu.make_async_remote_copy(
            src_ref=src, dst_ref=dst, send_sem=send, recv_sem=recv, device_id=device, device_id_type=MESH
        )

    token_copy = remote(
        hidden.at[:, pl.ds(pl.multiple_of((1 - c) * half, 128), half)],
        tokens.at[pl.ds(own_tokens, own_tokens)],
        small_send.at[1],
        small_recv.at[1],
        sib_dev,
    )
    token_copy.start()
    token_local = pltpu.make_async_copy(
        hidden.at[:, pl.ds(pl.multiple_of(c * half, 128), half)],
        tokens.at[pl.ds(0, own_tokens)],
        small_send.at[3],
    )
    token_local.start()

    def place(p):
        return jnp.where(r == 0, p, CHUNKS - 1 - p)

    def layer(j):
        if j == 0:
            return z
        at_end = jnp.where(z == 0, j, 3 - j)
        flip = (1, 3, 2)[j - 1]
        bits = z // 2, z % 2
        inner = ((bits[0] + flip // 2) % 2) * 2 + (bits[1] + flip % 2) % 2
        return jnp.where(middle, inner, at_end)

    def chunk(o, p):
        q = place(p)
        ref = blocks.at[o, pl.ds(pl.multiple_of(q * rows, rows), rows)]
        return ref, o * CHUNKS + q

    def move(o, p, sems, device):
        ref, n = chunk(o, p)
        return remote(ref, ref, sems.at[n], recv_sem.at[n], device)

    def z_move(o, p, way):
        return move(o, p, z_sem.at[way], up_dev if way == 0 else down_dev)

    lane = lax.broadcasted_iota(jnp.int32, (1, cols), 1)
    row_iota = lax.broadcasted_iota(jnp.int32, (side, cols), 0)
    col_iota = lax.broadcasted_iota(jnp.int32, (cols, cols), 0)
    left_lanes = lane < side
    second = jnp.where(lane % side >= side // 2, side, 0)

    def hot_rows(idx):
        return row_iota == (idx >> 6)

    def hot_cols(idx):
        return (col_iota == ((idx & (side - 1)) + second)).astype(jnp.bfloat16)

    def both_halves(value):
        return jnp.concatenate([value[:four], value[four:]], axis=1)

    def stacked(value):
        return jnp.concatenate([value[:, :cols], value[:, cols:]], axis=0)

    def inverse(coefficients):
        one, two = split(both_halves(coefficients))
        part = dot(one, basis[0]) + (dot(one, basis[1]) + dot(two, basis[0]))
        one, two = split(part)
        return stacked(dot(basis[3], one) + (dot(basis[3], two) + dot(basis[4], one)))

    def transform(value):
        one, two, three = split3(both_halves(value))
        part = dot(one, basis[3]) + (
            (dot(one, basis[4]) + dot(two, basis[3]))
            + (dot(one, basis[5]) + dot(two, basis[4]) + dot(three, basis[3]))
        )
        one, two, three = split3(part)
        return stacked(
            dot(basis[0], one)
            + (
                (dot(basis[0], two) + dot(basis[1], one))
                + (dot(basis[0], three) + dot(basis[1], two) + dot(basis[2], one))
            )
        )

    def tile_slice(q):
        return pl.ds(q * per if isinstance(q, int) else pl.multiple_of(q * per, per), per)

    def row_slice(q):
        return pl.ds(q * rows if isinstance(q, int) else pl.multiple_of(q * rows, rows), rows)

    def kept_copy(q):
        here = tile_slice(q)
        return remote(kept.at[here], kept_other.at[here], kept_send.at[q], kept_recv.at[q], y_dev)

    def forward(q):
        here = tile_slice(q)
        moment = decay_rate * momentum[here] + gradient[here].astype(jnp.float32)
        new_momentum[0, here] = moment
        spectrum = transform(moment.reshape(rows, cols))
        spectra[row_slice(q)] = spectrum
        idx = index[here]
        found = []
        for t in range(per):
            one = idx[t : t + 1]
            high, low = split(spectrum[t * side : (t + 1) * side])
            taken = dot(jnp.concatenate([high, low], axis=0), hot_cols(one))
            taken = taken[:side] + taken[side:]
            found.append(jnp.sum(jnp.where(hot_rows(one), taken, 0.0), axis=0, keepdims=True))
        kept[here] = jnp.concatenate(found, axis=0)
        kept_copy(q).start()

    own_block = 2 * z + x

    def step(p):
        q = place(p)
        here = tile_slice(q)
        kept_copy(q).wait_recv()
        idx = jnp.where(left_lanes, index[here], index_other[here])
        values = jnp.where(left_lanes, kept[here], kept_other[here]) * 0.5
        dense = []
        for t in range(per):
            one = idx[t : t + 1]
            high, low = split(jnp.where(hot_rows(one), values[t : t + 1], 0.0))
            put = dot_nt(jnp.concatenate([high, low], axis=0), hot_cols(one))
            tile = put[:side] + put[side:]
            energy = jnp.sum(tile * tile, axis=0, keepdims=True)
            left = jnp.sum(jnp.where(left_lanes, energy, 0.0), axis=1, keepdims=True)
            right = jnp.sum(jnp.where(left_lanes, 0.0, energy), axis=1, keepdims=True)
            energy = jnp.where(left_lanes, left, right)
            dense.append(tile * lax.rsqrt(energy / (side * side) + tiny_eps))
        raw = inverse(jnp.concatenate(dense, axis=0))
        direction = jnp.tanh(raw).astype(jnp.bfloat16).astype(jnp.float32)
        tiled = direction.reshape(per, side, cols)
        shown = jnp.where(r == 0, tiled[:, : side // 2], tiled[:, side // 2 :])
        update[here] = shown.astype(jnp.bfloat16)
        old = weight[here].astype(jnp.float32).reshape(rows, cols)
        blocks[own_block, row_slice(q)] = (old - step_size * direction).astype(jnp.bfloat16)

        if p < 4:

            @pl.when(up_ok)
            def _():
                z_move(own_block, p, 0).start()

            @pl.when(down_ok)
            def _():
                z_move(own_block, p, 1).start()

        if p < 3:
            move(own_block, p, x_sem, x_dev).start()

    loads[0].wait()
    loads[1].wait()
    spans = 2 * tiles
    diagonal = lax.broadcasted_iota(jnp.int32, (spans, spans), 0) == lax.broadcasted_iota(
        jnp.int32, (spans, spans), 1
    )
    limit = jnp.sum(jnp.where(diagonal, raw_count[...].astype(jnp.float32), 0.0), axis=1, keepdims=True)
    listed = raw_index[...]
    position = lax.broadcasted_iota(jnp.int32, listed.shape, 1).astype(jnp.float32)
    listed = jnp.where(position < limit, listed, -1)
    spread[...] = jnp.concatenate([listed] * 4, axis=1)
    index[...] = jnp.where(
        second > 0, spread[pl.ds(1, tiles, stride=2)], spread[pl.ds(0, tiles, stride=2)]
    )
    index_copy = remote(index, index_other, small_send.at[0], small_recv.at[0], y_dev)
    index_copy.start()
    for load in loads[2:5]:
        load.wait()
    forward(0)
    forward(CHUNKS - 1)
    forward(1)
    loads[5].wait()
    index_copy.wait_recv()
    step(0)
    forward(3)
    step(1)
    forward(2)
    step(2)
    step(3)
    step(4)

    def settle(q, carry):
        here = tile_slice(q)
        idx = index[here]
        spectrum = spectra[row_slice(q)]
        masks = []
        for t in range(per):
            one = idx[t : t + 1]
            hot = jnp.where(jnp.logical_and(hot_rows(one), left_lanes), 1.0, 0.0).astype(jnp.bfloat16)
            masks.append(dot_nt(hot, hot_cols(one)))
        own = jnp.where(jnp.concatenate(masks, axis=0) > 0.5, spectrum, 0.0)
        new_momentum[0, here] = new_momentum[0, here] - inverse(own).reshape(per, side, cols)
        return carry

    lax.fori_loop(0, CHUNKS, settle, 0)
    token_local.wait()
    token_copy.wait_recv()

    def arrived(o, p):
        move(o, p, x_sem, x_dev).wait_recv()

    def from_z(j, p):
        o = 2 * layer(j) + x
        arrived(o, p)
        below = layer(j) < z

        @pl.when(jnp.logical_and(below, up_ok))
        def _():
            z_move(o, p, 0).start()

        @pl.when(jnp.logical_and(jnp.logical_not(below), down_ok))
        def _():
            z_move(o, p, 1).start()

        if p < 3:
            move(o, p, x_sem, x_dev).start()
        if p == 0:
            move(o, p, y_sem, y_dev).start()

    def from_x(j, p):
        o = 2 * layer(j) + (1 - x)
        arrived(o, p)
        if p < 2:
            move(o, p, y_sem, y_dev).start()

    def part_copy(j):
        return remote(
            total.at[j, pl.ds(own_tokens, own_tokens)], partial.at[j], part_send.at[j], part_recv.at[j], sib_dev
        )

    def multiply(j):
        o = 2 * layer(j)

        def product(k):
            deep = pl.ds(pl.multiple_of(k * rows, rows), rows)
            both = jnp.concatenate([blocks[o, deep], blocks[o + 1, deep]], axis=1)
            return dot(tokens[:, deep], both)

        total[j] = product(0)

        def add(k, carry):
            total[j] += product(k)
            return carry

        lax.fori_loop(1, CHUNKS, add, 0)
        part_copy(j).start()

    for j in range(5):
        for p in range(4):
            if 1 <= j + 1 <= 3:
                from_z(j + 1, p)
            if j < 4 and p < 3:
                from_x(j, p)
        if j < 4:
            if j > 0:
                arrived(2 * layer(j) + x, 4)
            arrived(2 * layer(j) + (1 - x), 4)
            arrived(2 * layer(j) + (1 - x), 3)
            multiply(j)

    for j in range(4):
        part_copy(j).wait_recv()
        columns = pl.ds(pl.multiple_of(layer(j) * 2 * cols, 2 * cols), 2 * cols)
        keys[:, columns] = (total[j, :own_tokens] + partial[j]).astype(jnp.bfloat16)

    index_copy.wait_send()
    token_copy.wait_send()
    for q in range(CHUNKS):
        kept_copy(q).wait_send()
    for j in range(4):
        part_copy(j).wait_send()
        o = 2 * layer(j) + x
        below = layer(j) < z
        above = layer(j) > z
        goes_up = jnp.logical_and(jnp.logical_not(above), up_ok)
        goes_down = jnp.logical_and(jnp.logical_not(below), down_ok)
        for p in range(4):

            @pl.when(goes_up)
            def _():
                z_move(o, p, 0).wait_send()

            @pl.when(goes_down)
            def _():
                z_move(o, p, 1).wait_send()

            if p < 3:
                move(o, p, x_sem, x_dev).wait_send()
        if j > 0:
            move(o, 0, y_sem, y_dev).wait_send()
        for p in range(2):
            move(2 * layer(j) + (1 - x), p, y_sem, y_dev).wait_send()


def fused(hidden, weight, momentum, gradient, indices, counts):
    tiles, side, cols = weight.shape
    half = tiles * side
    own_tokens = hidden.shape[0]
    table = np.kron(np.eye(4), cosine_table(side))
    parts = []
    for rest in (table, table.T):
        for _ in range(3):
            parts.append(rest.astype(jnp.bfloat16))
            rest = rest - parts[-1].astype(np.float64)
    basis = jnp.asarray(np.stack(parts))
    vmem = pl.BlockSpec(memory_space=pltpu.VMEM)
    number = 8 * CHUNKS
    dma = pltpu.SemaphoreType.DMA
    keys, update, new_momentum = pl.pallas_call(
        fused_kernel,
        out_shape=(
            jax.ShapeDtypeStruct((own_tokens, 8 * cols), jnp.bfloat16),
            jax.ShapeDtypeStruct((tiles, side // 2, cols), jnp.bfloat16),
            jax.ShapeDtypeStruct(momentum.shape, jnp.float32),
        ),
        in_specs=[pl.BlockSpec(memory_space=pl.ANY)] * 7,
        out_specs=(vmem, vmem, vmem),
        scratch_shapes=[
            pltpu.VMEM((8, half, cols), jnp.bfloat16),
            pltpu.VMEM((2 * own_tokens, half), jnp.bfloat16),
            pltpu.VMEM((4, 2 * own_tokens, 2 * cols), jnp.float32),
            pltpu.VMEM((4, own_tokens, 2 * cols), jnp.float32),
            pltpu.VMEM((half, cols), jnp.float32),
            pltpu.VMEM((tiles, cols), jnp.float32),
            pltpu.VMEM((tiles, cols), jnp.float32),
            pltpu.VMEM((tiles, cols), jnp.int32),
            pltpu.VMEM((tiles, cols), jnp.int32),
            pltpu.VMEM(weight.shape, weight.dtype),
            pltpu.VMEM(momentum.shape[1:], momentum.dtype),
            pltpu.VMEM(gradient.shape[1:], gradient.dtype),
            pltpu.VMEM(basis.shape, basis.dtype),
            pltpu.VMEM(indices.shape[1:], indices.dtype),
            pltpu.VMEM(counts.shape, counts.dtype),
            pltpu.VMEM((2 * tiles, cols), jnp.int32),
            dma((6,)),
            dma((number,)),
            dma((2, number)),
            dma((number,)),
            dma((number,)),
            dma((4,)),
            dma((3,)),
            dma((CHUNKS,)),
            dma((CHUNKS,)),
            dma((4,)),
            dma((4,)),
        ],
        compiler_params=pltpu.CompilerParams(
            collective_id=0, has_side_effects=True, vmem_limit_bytes=60 * 1024 * 1024
        ),
    )(
        hidden,
        weight,
        momentum,
        gradient,
        indices,
        counts,
        basis,
    )
    return keys, update, new_momentum


finest_numeric_accuracy = lax.Precision.HIGHEST


def dct_table(length):
    wave_number = jnp.arange(length, dtype=jnp.float32)[:, None]
    position = jnp.arange(length, dtype=jnp.float32)[None, :]
    dct_rows = jnp.cos(jnp.pi * (2.0 * position + 1.0) * wave_number / (2.0 * length)) * jnp.sqrt(
        2.0 / length
    )
    return jnp.where(wave_number == 0.0, dct_rows * jnp.sqrt(0.5), dct_rows)


def make_pair(dct_rows):
    empty_square_tile = jnp.zeros_like(dct_rows)
    upper_half = jnp.concatenate([dct_rows, empty_square_tile], axis=1)
    lower_half = jnp.concatenate([empty_square_tile, dct_rows], axis=1)
    return jnp.concatenate([upper_half, lower_half], axis=0)


def to_spectrum(tile_data, row_basis_operator, paired_cosine_matrix):
    partial_transform = jnp.einsum(
        "ka,tab->tkb", row_basis_operator, tile_data, precision=finest_numeric_accuracy
    )
    return jnp.einsum(
        "tkb,cb->tkc", partial_transform, paired_cosine_matrix, precision=finest_numeric_accuracy
    )


def from_spectrum(tile_frequency_coefficients, row_basis_operator, paired_cosine_matrix):
    partial_transform = jnp.einsum(
        "yh,kyi->khi",
        row_basis_operator,
        tile_frequency_coefficients,
        precision=finest_numeric_accuracy,
    )
    return jnp.einsum(
        "pln,ns->pls", partial_transform, paired_cosine_matrix, precision=finest_numeric_accuracy
    )


def plain(hidden, weight, momentum, gradient, indices, counts):
    tiles_dev, block_side, tile_cols = weight.shape
    kept_count = indices.shape[2]
    replicas = lax.axis_size("rep")
    group_size = lax.axis_size("fsdp")
    all_tiles = tiles_dev * group_size
    width = hidden.shape[1]
    dct_rows = dct_table(block_side)
    paired_cosine_matrix = make_pair(dct_rows)
    moment = decay_rate * momentum[0] + gradient[0].astype(jnp.float32)
    tile_frequency_coefficients = to_spectrum(moment, dct_rows, paired_cosine_matrix)
    span_ids = jnp.arange(2 * tiles_dev, dtype=jnp.int32)[:, None]
    places = (
        span_ids // 2 * (block_side * tile_cols)
        + indices[0] // block_side * tile_cols
        + span_ids % 2 * block_side
        + indices[0] % block_side
    )
    picked = tile_frequency_coefficients.reshape(-1)[places]
    is_live = jnp.arange(kept_count, dtype=jnp.int32)[None, :] < counts[0][:, None]
    kept_values = jnp.where(is_live, picked, jnp.zeros_like(picked))
    flat_size = tiles_dev * block_side * tile_cols
    own_spectra = (
        jnp.zeros((flat_size,), jnp.float32).at[places.reshape(-1)].add(kept_values.reshape(-1))
    )
    own_spectra = own_spectra.reshape(tiles_dev, block_side, tile_cols)
    new_momentum = (moment - from_spectrum(own_spectra, dct_rows, paired_cosine_matrix))[None]
    all_places, all_values = (
        lax.all_gather(places[None], "rep", axis=0, tiled=True),
        lax.all_gather(kept_values[None], "rep", axis=0, tiled=True),
    )
    shared = (
        jnp.zeros((flat_size,), jnp.float32).at[all_places.reshape(-1)].add(all_values.reshape(-1))
    )
    shared = shared.reshape(tiles_dev, block_side, tile_cols) / replicas
    energy = jnp.sum((shared * shared).reshape(tiles_dev, block_side, 2, block_side), axis=(1, 3))
    span_scale = jnp.sqrt(energy / (block_side * block_side) + tiny_eps)
    span_scale = jnp.repeat(span_scale, block_side, axis=1)[:, None, :]
    rows_rep = block_side // replicas
    row_first = lax.axis_index("rep") * rows_rep
    raw_descent_direction = from_spectrum(shared, dct_rows, paired_cosine_matrix)
    update = jnp.tanh(raw_descent_direction / span_scale).astype(jnp.bfloat16)
    revised_parameters = (
        weight.astype(jnp.float32) - step_size * update.astype(jnp.float32)
    ).astype(jnp.bfloat16)
    assembled = lax.all_gather(revised_parameters, "fsdp", axis=0, tiled=True)
    out_update = lax.dynamic_slice_in_dim(update, row_first, rows_rep, 1)
    out_blocks = all_tiles // (width // block_side)
    matrix = assembled.reshape(out_blocks, width // block_side, block_side, tile_cols).transpose(
        1, 2, 0, 3
    )
    matrix = matrix.reshape(width, out_blocks * tile_cols)
    key_states = jnp.dot(hidden, matrix, preferred_element_type=jnp.float32).astype(jnp.bfloat16)
    return (key_states, out_update, new_momentum)


def solution(mesh):
    in_specs = (
        P(("rep", "fsdp"), None),
        P("fsdp", None, None),
        P("rep", "fsdp", None, None),
        P("rep", "fsdp", None, None),
        P("rep", "fsdp", None),
        P("rep", "fsdp"),
    )
    out_specs = (P(("rep", "fsdp"), None), P("fsdp", "rep", None), P("rep", "fsdp", None, None))
    small = mesh.shape["rep"] == 2 and mesh.shape["fsdp"] == 16
    shards = fused if small else plain
    return jax.shard_map(shards, mesh=mesh, in_specs=in_specs, out_specs=out_specs, check_vma=False)
```

```python
import functools

import jax
import jax.numpy as jnp
import numpy as np
from jax import lax
from jax.experimental import pallas as pl
from jax.experimental.pallas import tpu as pltpu
from jax.sharding import PartitionSpec as P

decay_rate = 0.999
step_size = 0.01
tiny_eps = 1e-06
exact = lax.Precision.HIGHEST
MESH = pl.DeviceIdType.MESH
CHUNKS = 5


def cosine_table(length):
    wave = np.arange(length, dtype=np.float64)[:, None]
    place = np.arange(length, dtype=np.float64)[None, :]
    table = np.cos(np.pi * (2.0 * place + 1.0) * wave / (2.0 * length)) * np.sqrt(2.0 / length)
    return np.where(wave == 0.0, table * np.sqrt(0.5), table)


def split(value):
    high = value.astype(jnp.bfloat16)
    return high, (value - high.astype(jnp.float32)).astype(jnp.bfloat16)


def dot(a, b):
    return jnp.dot(a, b, preferred_element_type=jnp.float32)


def dot_nt(a, b):
    return lax.dot_general(a, b, (((1,), (1,)), ((), ())), preferred_element_type=jnp.float32)


def split3(value):
    high = value.astype(jnp.bfloat16)
    rest = value - high.astype(jnp.float32)
    middle = rest.astype(jnp.bfloat16)
    return high, middle, (rest - middle.astype(jnp.float32)).astype(jnp.bfloat16)


def fused_kernel(
    hidden,
    weight_hbm,
    momentum_hbm,
    gradient_hbm,
    indices,
    counts,
    basis_hbm,
    keys,
    update,
    new_momentum,
    blocks,
    tokens,
    total,
    partial,
    spectra,
    kept,
    kept_other,
    index_other,
    index,
    weight,
    momentum,
    gradient,
    basis,
    raw_index,
    raw_count,
    spread,
    load_sem,
    recv_sem,
    z_sem,
    x_sem,
    y_sem,
    small_send,
    small_recv,
    kept_send,
    kept_recv,
    part_send,
    part_recv,
):
    loads = [
        pltpu.make_async_copy(src, dst, load_sem.at[n])
        for n, (src, dst) in enumerate(
            (
                (indices.at[0], raw_index),
                (counts, raw_count),
                (basis_hbm, basis),
                (momentum_hbm.at[0], momentum),
                (gradient_hbm.at[0], gradient),
                (weight_hbm, weight),
            )
        )
    ]
    for load in loads:
        load.start()
    tiles, side, cols = weight.shape
    per = tiles // CHUNKS
    rows = per * side
    half = tiles * side
    own_tokens = hidden.shape[0]
    pair = 2 * side
    four = 4 * side

    r = lax.axis_index("rep")
    f = lax.axis_index("fsdp")
    z, x, c = f // 4, (f // 2) % 2, f % 2
    middle = jnp.logical_and(z > 0, z < 3)
    up_ok, down_ok = z < 3, z > 0
    y_dev = (1 - r, f)
    x_dev = (r, z * 4 + (1 - x) * 2 + c)
    sib_dev = (r, z * 4 + x * 2 + (1 - c))
    up_dev = (r, jnp.minimum(f + 4, 15 - 3 + f % 4))
    down_dev = (r, jnp.maximum(f - 4, f % 4))

    barrier = pltpu.get_barrier_semaphore()
    for device in (y_dev, x_dev, sib_dev):
        pl.semaphore_signal(barrier, inc=1, device_id=device, device_id_type=MESH)

    @pl.when(up_ok)
    def _():
        pl.semaphore_signal(barrier, inc=1, device_id=up_dev, device_id_type=MESH)

    @pl.when(down_ok)
    def _():
        pl.semaphore_signal(barrier, inc=1, device_id=down_dev, device_id_type=MESH)

    pl.semaphore_wait(barrier, jnp.where(middle, 5, 4))

    def remote(src, dst, send, recv, device):
        return pltpu.make_async_remote_copy(
            src_ref=src, dst_ref=dst, send_sem=send, recv_sem=recv, device_id=device, device_id_type=MESH
        )

    token_copy = remote(
        hidden.at[:, pl.ds(pl.multiple_of((1 - c) * half, 128), half)],
        tokens.at[pl.ds(own_tokens, own_tokens)],
        small_send.at[1],
        small_recv.at[1],
        sib_dev,
    )
    token_copy.start()
    token_local = pltpu.make_async_copy(
        hidden.at[:, pl.ds(pl.multiple_of(c * half, 128), half)],
        tokens.at[pl.ds(0, own_tokens)],
        small_send.at[3],
    )
    token_local.start()

    def place(p):
        return jnp.where(r == 0, p, CHUNKS - 1 - p)

    def layer(j):
        if j == 0:
            return z
        at_end = jnp.where(z == 0, j, 3 - j)
        flip = (1, 3, 2)[j - 1]
        bits = z // 2, z % 2
        inner = ((bits[0] + flip // 2) % 2) * 2 + (bits[1] + flip % 2) % 2
        return jnp.where(middle, inner, at_end)

    def chunk(o, p):
        q = place(p)
        ref = blocks.at[o, pl.ds(pl.multiple_of(q * rows, rows), rows)]
        return ref, o * CHUNKS + q

    def move(o, p, sems, device):
        ref, n = chunk(o, p)
        return remote(ref, ref, sems.at[n], recv_sem.at[n], device)

    def z_move(o, p, way):
        return move(o, p, z_sem.at[way], up_dev if way == 0 else down_dev)

    lane = lax.broadcasted_iota(jnp.int32, (1, cols), 1)
    row_iota = lax.broadcasted_iota(jnp.int32, (side, cols), 0)
    col_iota = lax.broadcasted_iota(jnp.int32, (cols, cols), 0)
    left_lanes = lane < side
    second = jnp.where(lane % side >= side // 2, side, 0)

    def hot_rows(idx):
        return row_iota == (idx >> 6)

    def hot_cols(idx):
        return (col_iota == ((idx & (side - 1)) + second)).astype(jnp.bfloat16)

    def both_halves(value):
        return jnp.concatenate([value[:four], value[four:]], axis=1)

    def stacked(value):
        return jnp.concatenate([value[:, :cols], value[:, cols:]], axis=0)

    def inverse(coefficients):
        one, two = split(both_halves(coefficients))
        part = dot(one, basis[0]) + (dot(one, basis[1]) + dot(two, basis[0]))
        one, two = split(part)
        return stacked(dot(basis[3], one) + (dot(basis[3], two) + dot(basis[4], one)))

    def transform(value):
        one, two, three = split3(both_halves(value))
        part = dot(one, basis[3]) + (
            (dot(one, basis[4]) + dot(two, basis[3]))
            + (dot(one, basis[5]) + dot(two, basis[4]) + dot(three, basis[3]))
        )
        one, two, three = split3(part)
        return stacked(
            dot(basis[0], one)
            + (
                (dot(basis[0], two) + dot(basis[1], one))
                + (dot(basis[0], three) + dot(basis[1], two) + dot(basis[2], one))
            )
        )

    def tile_slice(q):
        return pl.ds(q * per if isinstance(q, int) else pl.multiple_of(q * per, per), per)

    def row_slice(q):
        return pl.ds(q * rows if isinstance(q, int) else pl.multiple_of(q * rows, rows), rows)

    def kept_copy(q):
        here = tile_slice(q)
        return remote(kept.at[here], kept_other.at[here], kept_send.at[q], kept_recv.at[q], y_dev)

    def forward(q):
        here = tile_slice(q)
        moment = decay_rate * momentum[here] + gradient[here].astype(jnp.float32)
        new_momentum[0, here] = moment
        spectrum = transform(moment.reshape(rows, cols))
        spectra[row_slice(q)] = spectrum
        idx = index[here]
        found = []
        for t in range(per):
            one = idx[t : t + 1]
            high, low = split(spectrum[t * side : (t + 1) * side])
            taken = dot(jnp.concatenate([high, low], axis=0), hot_cols(one))
            taken = taken[:side] + taken[side:]
            found.append(jnp.sum(jnp.where(hot_rows(one), taken, 0.0), axis=0, keepdims=True))
        kept[here] = jnp.concatenate(found, axis=0)
        kept_copy(q).start()

    own_block = 2 * z + x

    def step(p):
        q = place(p)
        here = tile_slice(q)
        kept_copy(q).wait_recv()
        idx = jnp.where(left_lanes, index[here], index_other[here])
        values = jnp.where(left_lanes, kept[here], kept_other[here]) * 0.5
        dense = []
        for t in range(per):
            one = idx[t : t + 1]
            high, low = split(jnp.where(hot_rows(one), values[t : t + 1], 0.0))
            put = dot_nt(jnp.concatenate([high, low], axis=0), hot_cols(one))
            tile = put[:side] + put[side:]
            energy = jnp.sum(tile * tile, axis=0, keepdims=True)
            left = jnp.sum(jnp.where(left_lanes, energy, 0.0), axis=1, keepdims=True)
            right = jnp.sum(jnp.where(left_lanes, 0.0, energy), axis=1, keepdims=True)
            energy = jnp.where(left_lanes, left, right)
            dense.append(tile * lax.rsqrt(energy / (side * side) + tiny_eps))
        raw = inverse(jnp.concatenate(dense, axis=0))
        direction = jnp.tanh(raw).astype(jnp.bfloat16).astype(jnp.float32)
        tiled = direction.reshape(per, side, cols)
        shown = jnp.where(r == 0, tiled[:, : side // 2], tiled[:, side // 2 :])
        update[here] = shown.astype(jnp.bfloat16)
        old = weight[here].astype(jnp.float32).reshape(rows, cols)
        blocks[own_block, row_slice(q)] = (old - step_size * direction).astype(jnp.bfloat16)

        if p < 4:

            @pl.when(up_ok)
            def _():
                z_move(own_block, p, 0).start()

            @pl.when(down_ok)
            def _():
                z_move(own_block, p, 1).start()

        if p < 3:
            move(own_block, p, x_sem, x_dev).start()

    def arrived(o, p):
        move(o, p, x_sem, x_dev).wait_recv()

    def from_z(j, p):
        o = 2 * layer(j) + x
        arrived(o, p)
        below = layer(j) < z

        @pl.when(jnp.logical_and(below, up_ok))
        def _():
            z_move(o, p, 0).start()

        @pl.when(jnp.logical_and(jnp.logical_not(below), down_ok))
        def _():
            z_move(o, p, 1).start()

        if p < 3:
            move(o, p, x_sem, x_dev).start()
        if p == 0:
            move(o, p, y_sem, y_dev).start()

    def from_x(j, p):
        o = 2 * layer(j) + (1 - x)
        arrived(o, p)
        if p < 2:
            move(o, p, y_sem, y_dev).start()

    def settle(q):
        here = tile_slice(q)
        idx = index[here]
        spectrum = spectra[row_slice(q)]
        masks = []
        for t in range(per):
            one = idx[t : t + 1]
            hot = jnp.where(jnp.logical_and(hot_rows(one), left_lanes), 1.0, 0.0).astype(jnp.bfloat16)
            masks.append(dot_nt(hot, hot_cols(one)))
        own = jnp.where(jnp.concatenate(masks, axis=0) > 0.5, spectrum, 0.0)
        new_momentum[0, here] = new_momentum[0, here] - inverse(own).reshape(per, side, cols)

    loads[0].wait()
    loads[1].wait()
    listed = raw_index[...]
    position = lax.broadcasted_iota(jnp.int32, listed.shape, 0)
    spread[...] = jnp.full(spread.shape, -1, jnp.int32)
    spread[: listed.shape[0], : listed.shape[1]] = jnp.where(position < raw_count[...], listed, -1)
    spread[...] = jnp.transpose(jnp.concatenate([spread[: listed.shape[0]]] * 4, axis=0))
    index[...] = jnp.where(
        second > 0, spread[pl.ds(1, tiles, stride=2)], spread[pl.ds(0, tiles, stride=2)]
    )
    index_copy = remote(index, index_other, small_send.at[0], small_recv.at[0], y_dev)
    index_copy.start()
    for load in loads[2:5]:
        load.wait()
    forward(0)
    forward(CHUNKS - 1)
    forward(1)
    loads[5].wait()
    index_copy.wait_recv()
    step(0)
    forward(3)
    step(1)
    from_z(1, 0)
    from_x(0, 0)
    forward(2)
    step(2)
    from_z(1, 1)
    from_x(0, 1)
    step(3)
    from_z(1, 2)
    from_x(0, 2)
    step(4)
    from_z(1, 3)

    token_local.wait()
    token_copy.wait_recv()

    def part_copy(j):
        return remote(
            total.at[j, pl.ds(own_tokens, own_tokens)], partial.at[j], part_send.at[j], part_recv.at[j], sib_dev
        )

    def multiply(j):
        o = 2 * layer(j)

        def product(k):
            deep = pl.ds(pl.multiple_of(k * rows, rows), rows)
            both = jnp.concatenate([blocks[o, deep], blocks[o + 1, deep]], axis=1)
            return dot(tokens[:, deep], both)

        total[j] = product(0)

        def add(k, carry):
            total[j] += product(k)
            return carry

        lax.fori_loop(1, CHUNKS, add, 0)
        part_copy(j).start()

    for j in range(4):
        if j > 0:
            for p in range(4):
                if j < 3:
                    from_z(j + 1, p)
                if p < 3:
                    from_x(j, p)
                if j < 3 and 4 * (j - 1) + p < CHUNKS:
                    settle(4 * (j - 1) + p)
            arrived(2 * layer(j) + x, 4)
        arrived(2 * layer(j) + (1 - x), 4)
        arrived(2 * layer(j) + (1 - x), 3)
        multiply(j)

    for j in range(4):
        part_copy(j).wait_recv()
        columns = pl.ds(pl.multiple_of(layer(j) * 2 * cols, 2 * cols), 2 * cols)
        keys[:, columns] = (total[j, :own_tokens] + partial[j]).astype(jnp.bfloat16)

    index_copy.wait_send()
    token_copy.wait_send()
    for q in range(CHUNKS):
        kept_copy(q).wait_send()
    for j in range(4):
        part_copy(j).wait_send()
        o = 2 * layer(j) + x
        below = layer(j) < z
        above = layer(j) > z
        goes_up = jnp.logical_and(jnp.logical_not(above), up_ok)
        goes_down = jnp.logical_and(jnp.logical_not(below), down_ok)
        for p in range(4):

            @pl.when(goes_up)
            def _():
                z_move(o, p, 0).wait_send()

            @pl.when(goes_down)
            def _():
                z_move(o, p, 1).wait_send()

            if p < 3:
                move(o, p, x_sem, x_dev).wait_send()
        if j > 0:
            move(o, 0, y_sem, y_dev).wait_send()
        for p in range(2):
            move(2 * layer(j) + (1 - x), p, y_sem, y_dev).wait_send()


def fused(hidden, weight, momentum, gradient, indices, counts):
    tiles, side, cols = weight.shape
    kept_count = indices.shape[2]
    half = tiles * side
    own_tokens = hidden.shape[0]
    table = np.kron(np.eye(4), cosine_table(side))
    parts = []
    for rest in (table, table.T):
        for _ in range(3):
            parts.append(rest.astype(jnp.bfloat16))
            rest = rest - parts[-1].astype(np.float64)
    basis = jnp.asarray(np.stack(parts))
    vmem = pl.BlockSpec(memory_space=pltpu.VMEM)
    number = 8 * CHUNKS
    dma = pltpu.SemaphoreType.DMA
    keys, update, new_momentum = pl.pallas_call(
        fused_kernel,
        out_shape=(
            jax.ShapeDtypeStruct((own_tokens, 8 * cols), jnp.bfloat16),
            jax.ShapeDtypeStruct((tiles, side // 2, cols), jnp.bfloat16),
            jax.ShapeDtypeStruct(momentum.shape, jnp.float32),
        ),
        in_specs=[pl.BlockSpec(memory_space=pltpu.HBM)] * 7,
        out_specs=(vmem, vmem, vmem),
        scratch_shapes=[
            pltpu.VMEM((8, half, cols), jnp.bfloat16),
            pltpu.VMEM((2 * own_tokens, half), jnp.bfloat16),
            pltpu.VMEM((4, 2 * own_tokens, 2 * cols), jnp.float32),
            pltpu.VMEM((4, own_tokens, 2 * cols), jnp.float32),
            pltpu.VMEM((half, cols), jnp.float32),
            pltpu.VMEM((tiles, cols), jnp.float32),
            pltpu.VMEM((tiles, cols), jnp.float32),
            pltpu.VMEM((tiles, cols), jnp.int32),
            pltpu.VMEM((tiles, cols), jnp.int32),
            pltpu.VMEM(weight.shape, weight.dtype),
            pltpu.VMEM(momentum.shape[1:], momentum.dtype),
            pltpu.VMEM(gradient.shape[1:], gradient.dtype),
            pltpu.VMEM(basis.shape, basis.dtype),
            pltpu.VMEM((kept_count, 2 * tiles), indices.dtype),
            pltpu.VMEM(counts.shape, counts.dtype),
            pltpu.VMEM((cols, cols), jnp.int32),
            dma((6,)),
            dma((number,)),
            dma((2, number)),
            dma((number,)),
            dma((number,)),
            dma((4,)),
            dma((3,)),
            dma((CHUNKS,)),
            dma((CHUNKS,)),
            dma((4,)),
            dma((4,)),
        ],
        compiler_params=pltpu.CompilerParams(
            collective_id=0, has_side_effects=True, vmem_limit_bytes=53 * 1024 * 1024
        ),
    )(
        hidden,
        weight,
        momentum,
        gradient,
        jnp.swapaxes(indices, 1, 2),
        counts,
        basis,
    )
    return keys, update, new_momentum


finest_numeric_accuracy = lax.Precision.HIGHEST


def dct_table(length):
    wave_number = jnp.arange(length, dtype=jnp.float32)[:, None]
    position = jnp.arange(length, dtype=jnp.float32)[None, :]
    dct_rows = jnp.cos(jnp.pi * (2.0 * position + 1.0) * wave_number / (2.0 * length)) * jnp.sqrt(
        2.0 / length
    )
    return jnp.where(wave_number == 0.0, dct_rows * jnp.sqrt(0.5), dct_rows)


def make_pair(dct_rows):
    empty_square_tile = jnp.zeros_like(dct_rows)
    upper_half = jnp.concatenate([dct_rows, empty_square_tile], axis=1)
    lower_half = jnp.concatenate([empty_square_tile, dct_rows], axis=1)
    return jnp.concatenate([upper_half, lower_half], axis=0)


def to_spectrum(tile_data, row_basis_operator, paired_cosine_matrix):
    partial_transform = jnp.einsum(
        "ka,tab->tkb", row_basis_operator, tile_data, precision=finest_numeric_accuracy
    )
    return jnp.einsum(
        "tkb,cb->tkc", partial_transform, paired_cosine_matrix, precision=finest_numeric_accuracy
    )


def from_spectrum(tile_frequency_coefficients, row_basis_operator, paired_cosine_matrix):
    partial_transform = jnp.einsum(
        "yh,kyi->khi",
        row_basis_operator,
        tile_frequency_coefficients,
        precision=finest_numeric_accuracy,
    )
    return jnp.einsum(
        "pln,ns->pls", partial_transform, paired_cosine_matrix, precision=finest_numeric_accuracy
    )


def plain(hidden, weight, momentum, gradient, indices, counts):
    tiles_dev, block_side, tile_cols = weight.shape
    kept_count = indices.shape[2]
    replicas = lax.axis_size("rep")
    group_size = lax.axis_size("fsdp")
    all_tiles = tiles_dev * group_size
    width = hidden.shape[1]
    dct_rows = dct_table(block_side)
    paired_cosine_matrix = make_pair(dct_rows)
    moment = decay_rate * momentum[0] + gradient[0].astype(jnp.float32)
    tile_frequency_coefficients = to_spectrum(moment, dct_rows, paired_cosine_matrix)
    span_ids = jnp.arange(2 * tiles_dev, dtype=jnp.int32)[:, None]
    places = (
        span_ids // 2 * (block_side * tile_cols)
        + indices[0] // block_side * tile_cols
        + span_ids % 2 * block_side
        + indices[0] % block_side
    )
    picked = tile_frequency_coefficients.reshape(-1)[places]
    is_live = jnp.arange(kept_count, dtype=jnp.int32)[None, :] < counts[0][:, None]
    kept_values = jnp.where(is_live, picked, jnp.zeros_like(picked))
    flat_size = tiles_dev * block_side * tile_cols
    own_spectra = (
        jnp.zeros((flat_size,), jnp.float32).at[places.reshape(-1)].add(kept_values.reshape(-1))
    )
    own_spectra = own_spectra.reshape(tiles_dev, block_side, tile_cols)
    new_momentum = (moment - from_spectrum(own_spectra, dct_rows, paired_cosine_matrix))[None]
    all_places, all_values = (
        lax.all_gather(places[None], "rep", axis=0, tiled=True),
        lax.all_gather(kept_values[None], "rep", axis=0, tiled=True),
    )
    shared = (
        jnp.zeros((flat_size,), jnp.float32).at[all_places.reshape(-1)].add(all_values.reshape(-1))
    )
    shared = shared.reshape(tiles_dev, block_side, tile_cols) / replicas
    energy = jnp.sum((shared * shared).reshape(tiles_dev, block_side, 2, block_side), axis=(1, 3))
    span_scale = jnp.sqrt(energy / (block_side * block_side) + tiny_eps)
    span_scale = jnp.repeat(span_scale, block_side, axis=1)[:, None, :]
    rows_rep = block_side // replicas
    row_first = lax.axis_index("rep") * rows_rep
    raw_descent_direction = from_spectrum(shared, dct_rows, paired_cosine_matrix)
    update = jnp.tanh(raw_descent_direction / span_scale).astype(jnp.bfloat16)
    revised_parameters = (
        weight.astype(jnp.float32) - step_size * update.astype(jnp.float32)
    ).astype(jnp.bfloat16)
    assembled = lax.all_gather(revised_parameters, "fsdp", axis=0, tiled=True)
    out_update = lax.dynamic_slice_in_dim(update, row_first, rows_rep, 1)
    out_blocks = all_tiles // (width // block_side)
    matrix = assembled.reshape(out_blocks, width // block_side, block_side, tile_cols).transpose(
        1, 2, 0, 3
    )
    matrix = matrix.reshape(width, out_blocks * tile_cols)
    key_states = jnp.dot(hidden, matrix, preferred_element_type=jnp.float32).astype(jnp.bfloat16)
    return (key_states, out_update, new_momentum)


def solution(mesh):
    in_specs = (
        P(("rep", "fsdp"), None),
        P("fsdp", None, None),
        P("rep", "fsdp", None, None),
        P("rep", "fsdp", None, None),
        P("rep", "fsdp", None),
        P("rep", "fsdp"),
    )
    out_specs = (P(("rep", "fsdp"), None), P("fsdp", "rep", None), P("rep", "fsdp", None, None))
    small = mesh.shape["rep"] == 2 and mesh.shape["fsdp"] == 16
    shards = fused if small else plain
    return jax.shard_map(shards, mesh=mesh, in_specs=in_specs, out_specs=out_specs, check_vma=False)
```

```python
import functools

import jax
import jax.numpy as jnp
import numpy as np
from jax import lax
from jax.experimental import pallas as pl
from jax.experimental.pallas import tpu as pltpu
from jax.sharding import PartitionSpec as P

decay_rate = 0.999
step_size = 0.01
tiny_eps = 1e-06
exact = lax.Precision.HIGHEST
MESH = pl.DeviceIdType.MESH
CHUNKS = 5


def cosine_table(length):
    wave = np.arange(length, dtype=np.float64)[:, None]
    place = np.arange(length, dtype=np.float64)[None, :]
    table = np.cos(np.pi * (2.0 * place + 1.0) * wave / (2.0 * length)) * np.sqrt(2.0 / length)
    return np.where(wave == 0.0, table * np.sqrt(0.5), table)


def split(value):
    high = value.astype(jnp.bfloat16)
    return high, (value - high.astype(jnp.float32)).astype(jnp.bfloat16)


def dot(a, b):
    return jnp.dot(a, b, preferred_element_type=jnp.float32)


def dot_nt(a, b):
    return lax.dot_general(a, b, (((1,), (1,)), ((), ())), preferred_element_type=jnp.float32)


def split3(value):
    high = value.astype(jnp.bfloat16)
    rest = value - high.astype(jnp.float32)
    middle = rest.astype(jnp.bfloat16)
    return high, middle, (rest - middle.astype(jnp.float32)).astype(jnp.bfloat16)


def fused_kernel(
    hidden,
    weight_hbm,
    momentum_hbm,
    gradient_hbm,
    indices,
    counts,
    basis_hbm,
    keys,
    update,
    new_momentum,
    blocks,
    tokens,
    total,
    partial,
    spectra,
    kept,
    kept_other,
    index_other,
    index,
    weight,
    momentum,
    gradient,
    basis,
    raw_index,
    raw_count,
    spread,
    load_sem,
    recv_sem,
    z_sem,
    x_sem,
    y_sem,
    small_send,
    small_recv,
    kept_send,
    kept_recv,
    part_send,
    part_recv,
):
    loads = [
        pltpu.make_async_copy(src, dst, load_sem.at[n])
        for n, (src, dst) in enumerate(
            (
                (indices.at[0], raw_index),
                (counts, raw_count),
                (basis_hbm, basis),
                (momentum_hbm.at[0], momentum),
                (gradient_hbm.at[0], gradient),
                (weight_hbm, weight),
            )
        )
    ]
    for load in loads:
        load.start()
    tiles, side, cols = weight.shape
    per = tiles // CHUNKS
    rows = per * side
    half = tiles * side
    own_tokens = hidden.shape[0]
    pair = 2 * side
    four = 4 * side

    r = lax.axis_index("rep")
    f = lax.axis_index("fsdp")
    z, x, c = f // 4, (f // 2) % 2, f % 2
    middle = jnp.logical_and(z > 0, z < 3)
    up_ok, down_ok = z < 3, z > 0
    y_dev = (1 - r, f)
    x_dev = (r, z * 4 + (1 - x) * 2 + c)
    sib_dev = (r, z * 4 + x * 2 + (1 - c))
    up_dev = (r, jnp.minimum(f + 4, 15 - 3 + f % 4))
    down_dev = (r, jnp.maximum(f - 4, f % 4))

    barrier = pltpu.get_barrier_semaphore()
    for device in (y_dev, x_dev, sib_dev):
        pl.semaphore_signal(barrier, inc=1, device_id=device, device_id_type=MESH)

    @pl.when(up_ok)
    def _():
        pl.semaphore_signal(barrier, inc=1, device_id=up_dev, device_id_type=MESH)

    @pl.when(down_ok)
    def _():
        pl.semaphore_signal(barrier, inc=1, device_id=down_dev, device_id_type=MESH)

    pl.semaphore_wait(barrier, jnp.where(middle, 5, 4))

    def remote(src, dst, send, recv, device):
        return pltpu.make_async_remote_copy(
            src_ref=src, dst_ref=dst, send_sem=send, recv_sem=recv, device_id=device, device_id_type=MESH
        )

    token_copy = remote(
        hidden.at[:, pl.ds(pl.multiple_of((1 - c) * half, 128), half)],
        tokens.at[pl.ds(own_tokens, own_tokens)],
        small_send.at[1],
        small_recv.at[1],
        sib_dev,
    )
    token_copy.start()
    token_local = pltpu.make_async_copy(
        hidden.at[:, pl.ds(pl.multiple_of(c * half, 128), half)],
        tokens.at[pl.ds(0, own_tokens)],
        small_send.at[3],
    )
    token_local.start()

    def place(p):
        return jnp.where(r == 0, p, CHUNKS - 1 - p)

    def layer(j):
        if j == 0:
            return z
        at_end = jnp.where(z == 0, j, 3 - j)
        flip = (1, 3, 2)[j - 1]
        bits = z // 2, z % 2
        inner = ((bits[0] + flip // 2) % 2) * 2 + (bits[1] + flip % 2) % 2
        return jnp.where(middle, inner, at_end)

    def chunk(o, p):
        q = place(p)
        ref = blocks.at[o, pl.ds(pl.multiple_of(q * rows, rows), rows)]
        return ref, o * CHUNKS + q

    def move(o, p, sems, device):
        ref, n = chunk(o, p)
        return remote(ref, ref, sems.at[n], recv_sem.at[n], device)

    def z_move(o, p, way):
        return move(o, p, z_sem.at[way], up_dev if way == 0 else down_dev)

    lane = lax.broadcasted_iota(jnp.int32, (1, cols), 1)
    row_iota = lax.broadcasted_iota(jnp.int32, (side, cols), 0)
    col_iota = lax.broadcasted_iota(jnp.int32, (cols, cols), 0)
    left_lanes = lane < side
    second = jnp.where(lane % side >= side // 2, side, 0)

    def hot_rows(idx):
        return row_iota == (idx >> 6)

    def hot_cols(idx):
        return (col_iota == ((idx & (side - 1)) + second)).astype(jnp.bfloat16)

    def both_halves(value):
        return jnp.concatenate([value[:four], value[four:]], axis=1)

    def stacked(value):
        return jnp.concatenate([value[:, :cols], value[:, cols:]], axis=0)

    def inverse(coefficients):
        one, two = split(both_halves(coefficients))
        part = dot(one, basis[0]) + (dot(one, basis[1]) + dot(two, basis[0]))
        one, two = split(part)
        return stacked(dot(basis[3], one) + (dot(basis[3], two) + dot(basis[4], one)))

    def transform(value):
        one, two, three = split3(both_halves(value))
        part = dot(one, basis[3]) + (
            (dot(one, basis[4]) + dot(two, basis[3]))
            + (dot(one, basis[5]) + dot(two, basis[4]) + dot(three, basis[3]))
        )
        one, two, three = split3(part)
        return stacked(
            dot(basis[0], one)
            + (
                (dot(basis[0], two) + dot(basis[1], one))
                + (dot(basis[0], three) + dot(basis[1], two) + dot(basis[2], one))
            )
        )

    def tile_slice(q):
        return pl.ds(q * per if isinstance(q, int) else pl.multiple_of(q * per, per), per)

    def row_slice(q):
        return pl.ds(q * rows if isinstance(q, int) else pl.multiple_of(q * rows, rows), rows)

    def kept_copy(q):
        here = tile_slice(q)
        return remote(kept.at[here], kept_other.at[here], kept_send.at[q], kept_recv.at[q], y_dev)

    def forward(q):
        here = tile_slice(q)
        moment = decay_rate * momentum[here] + gradient[here].astype(jnp.float32)
        new_momentum[0, here] = moment
        spectrum = transform(moment.reshape(rows, cols))
        spectra[row_slice(q)] = spectrum
        idx = index[here]
        found = []
        for t in range(per):
            one = idx[t : t + 1]
            high, low = split(spectrum[t * side : (t + 1) * side])
            taken = dot(jnp.concatenate([high, low], axis=0), hot_cols(one))
            taken = taken[:side] + taken[side:]
            found.append(jnp.sum(jnp.where(hot_rows(one), taken, 0.0), axis=0, keepdims=True))
        kept[here] = jnp.concatenate(found, axis=0)
        kept_copy(q).start()

    own_block = 2 * z + x

    def step(p):
        q = place(p)
        here = tile_slice(q)
        kept_copy(q).wait_recv()
        idx = jnp.where(left_lanes, index[here], index_other[here])
        values = jnp.where(left_lanes, kept[here], kept_other[here]) * 0.5
        dense = []
        for t in range(per):
            one = idx[t : t + 1]
            high, low = split(jnp.where(hot_rows(one), values[t : t + 1], 0.0))
            put = dot_nt(jnp.concatenate([high, low], axis=0), hot_cols(one))
            tile = put[:side] + put[side:]
            energy = jnp.sum(tile * tile, axis=0, keepdims=True)
            left = jnp.sum(jnp.where(left_lanes, energy, 0.0), axis=1, keepdims=True)
            right = jnp.sum(jnp.where(left_lanes, 0.0, energy), axis=1, keepdims=True)
            energy = jnp.where(left_lanes, left, right)
            dense.append(tile * lax.rsqrt(energy / (side * side) + tiny_eps))
        raw = inverse(jnp.concatenate(dense, axis=0))
        direction = jnp.tanh(raw).astype(jnp.bfloat16).astype(jnp.float32)
        tiled = direction.reshape(per, side, cols)
        shown = jnp.where(r == 0, tiled[:, : side // 2], tiled[:, side // 2 :])
        update[here] = shown.astype(jnp.bfloat16)
        old = weight[here].astype(jnp.float32).reshape(rows, cols)
        blocks[own_block, row_slice(q)] = (old - step_size * direction).astype(jnp.bfloat16)

        if p < 4:

            @pl.when(up_ok)
            def _():
                z_move(own_block, p, 0).start()

            @pl.when(down_ok)
            def _():
                z_move(own_block, p, 1).start()

        if p < 3:
            move(own_block, p, x_sem, x_dev).start()

    def arrived(o, p):
        move(o, p, x_sem, x_dev).wait_recv()

    def from_z(level, p):
        o = 2 * level + x
        arrived(o, p)
        below = level < z

        @pl.when(jnp.logical_and(below, up_ok))
        def _():
            z_move(o, p, 0).start()

        @pl.when(jnp.logical_and(jnp.logical_not(below), down_ok))
        def _():
            z_move(o, p, 1).start()

        if p < 3:
            move(o, p, x_sem, x_dev).start()
        if p == 0:
            move(o, p, y_sem, y_dev).start()

    def from_x(j, p):
        o = 2 * layer(j) + (1 - x)
        arrived(o, p)
        if p < 2:
            move(o, p, y_sem, y_dev).start()

    def settle(q):
        here = tile_slice(q)
        idx = index[here]
        spectrum = spectra[row_slice(q)]
        masks = []
        for t in range(per):
            one = idx[t : t + 1]
            hot = jnp.where(jnp.logical_and(hot_rows(one), left_lanes), 1.0, 0.0).astype(jnp.bfloat16)
            masks.append(dot_nt(hot, hot_cols(one)))
        own = jnp.where(jnp.concatenate(masks, axis=0) > 0.5, spectrum, 0.0)
        new_momentum[0, here] = new_momentum[0, here] - inverse(own).reshape(per, side, cols)

    def near(p):
        from_z(layer(1), p)

        @pl.when(middle)
        def _():
            from_z(layer(2), p)

    def far(p):
        from_z(jnp.where(middle, layer(3), layer(2)), p)

    def farthest(p):
        @pl.when(jnp.logical_not(middle))
        def _():
            from_z(layer(3), p)

    loads[0].wait()
    loads[1].wait()
    listed = raw_index[...]
    position = lax.broadcasted_iota(jnp.int32, listed.shape, 0)
    spread[...] = jnp.full(spread.shape, -1, jnp.int32)
    spread[: listed.shape[0], : listed.shape[1]] = jnp.where(position < raw_count[...], listed, -1)
    spread[...] = jnp.transpose(jnp.concatenate([spread[: listed.shape[0]]] * 4, axis=0))
    index[...] = jnp.where(
        second > 0, spread[pl.ds(1, tiles, stride=2)], spread[pl.ds(0, tiles, stride=2)]
    )
    index_copy = remote(index, index_other, small_send.at[0], small_recv.at[0], y_dev)
    index_copy.start()
    for load in loads[2:5]:
        load.wait()
    forward(0)
    forward(CHUNKS - 1)
    forward(1)
    loads[5].wait()
    index_copy.wait_recv()
    step(0)
    forward(3)
    step(1)
    near(0)
    from_x(0, 0)
    forward(2)
    step(2)
    near(1)
    from_x(0, 1)
    step(3)
    near(2)
    from_x(0, 2)
    step(4)
    near(3)

    token_local.wait()
    token_copy.wait_recv()

    def part_copy(j):
        return remote(
            total.at[j, pl.ds(own_tokens, own_tokens)], partial.at[j], part_send.at[j], part_recv.at[j], sib_dev
        )

    def multiply(j):
        o = 2 * layer(j)

        def product(k):
            deep = pl.ds(pl.multiple_of(k * rows, rows), rows)
            both = jnp.concatenate([blocks[o, deep], blocks[o + 1, deep]], axis=1)
            return dot(tokens[:, deep], both)

        total[j] = product(0)

        def add(k, carry):
            total[j] += product(k)
            return carry

        lax.fori_loop(1, CHUNKS, add, 0)
        part_copy(j).start()

    for j in range(4):
        if j > 0:
            for p in range(4):
                if j < 3:
                    (far, farthest)[j - 1](p)
                if p < 3:
                    from_x(j, p)
                if j < 3 and 4 * (j - 1) + p < CHUNKS:
                    settle(4 * (j - 1) + p)
            arrived(2 * layer(j) + x, 4)
        arrived(2 * layer(j) + (1 - x), 4)
        arrived(2 * layer(j) + (1 - x), 3)
        multiply(j)

    for j in range(4):
        part_copy(j).wait_recv()
        columns = pl.ds(pl.multiple_of(layer(j) * 2 * cols, 2 * cols), 2 * cols)
        keys[:, columns] = (total[j, :own_tokens] + partial[j]).astype(jnp.bfloat16)

    index_copy.wait_send()
    token_copy.wait_send()
    for q in range(CHUNKS):
        kept_copy(q).wait_send()
    for j in range(4):
        part_copy(j).wait_send()
        o = 2 * layer(j) + x
        below = layer(j) < z
        above = layer(j) > z
        goes_up = jnp.logical_and(jnp.logical_not(above), up_ok)
        goes_down = jnp.logical_and(jnp.logical_not(below), down_ok)
        for p in range(4):

            @pl.when(goes_up)
            def _():
                z_move(o, p, 0).wait_send()

            @pl.when(goes_down)
            def _():
                z_move(o, p, 1).wait_send()

            if p < 3:
                move(o, p, x_sem, x_dev).wait_send()
        if j > 0:
            move(o, 0, y_sem, y_dev).wait_send()
        for p in range(2):
            move(2 * layer(j) + (1 - x), p, y_sem, y_dev).wait_send()


def fused(hidden, weight, momentum, gradient, indices, counts):
    tiles, side, cols = weight.shape
    kept_count = indices.shape[2]
    half = tiles * side
    own_tokens = hidden.shape[0]
    table = np.kron(np.eye(4), cosine_table(side))
    parts = []
    for rest in (table, table.T):
        for _ in range(3):
            parts.append(rest.astype(jnp.bfloat16))
            rest = rest - parts[-1].astype(np.float64)
    basis = jnp.asarray(np.stack(parts))
    vmem = pl.BlockSpec(memory_space=pltpu.VMEM)
    number = 8 * CHUNKS
    dma = pltpu.SemaphoreType.DMA
    keys, update, new_momentum = pl.pallas_call(
        fused_kernel,
        out_shape=(
            jax.ShapeDtypeStruct((own_tokens, 8 * cols), jnp.bfloat16),
            jax.ShapeDtypeStruct((tiles, side // 2, cols), jnp.bfloat16),
            jax.ShapeDtypeStruct(momentum.shape, jnp.float32),
        ),
        in_specs=[pl.BlockSpec(memory_space=pltpu.HBM)] * 7,
        out_specs=(vmem, vmem, vmem),
        scratch_shapes=[
            pltpu.VMEM((8, half, cols), jnp.bfloat16),
            pltpu.VMEM((2 * own_tokens, half), jnp.bfloat16),
            pltpu.VMEM((4, 2 * own_tokens, 2 * cols), jnp.float32),
            pltpu.VMEM((4, own_tokens, 2 * cols), jnp.float32),
            pltpu.VMEM((half, cols), jnp.float32),
            pltpu.VMEM((tiles, cols), jnp.float32),
            pltpu.VMEM((tiles, cols), jnp.float32),
            pltpu.VMEM((tiles, cols), jnp.int32),
            pltpu.VMEM((tiles, cols), jnp.int32),
            pltpu.VMEM(weight.shape, weight.dtype),
            pltpu.VMEM(momentum.shape[1:], momentum.dtype),
            pltpu.VMEM(gradient.shape[1:], gradient.dtype),
            pltpu.VMEM(basis.shape, basis.dtype),
            pltpu.VMEM((kept_count, 2 * tiles), indices.dtype),
            pltpu.VMEM(counts.shape, counts.dtype),
            pltpu.VMEM((cols, cols), jnp.int32),
            dma((6,)),
            dma((number,)),
            dma((2, number)),
            dma((number,)),
            dma((number,)),
            dma((4,)),
            dma((3,)),
            dma((CHUNKS,)),
            dma((CHUNKS,)),
            dma((4,)),
            dma((4,)),
        ],
        compiler_params=pltpu.CompilerParams(
            collective_id=0, has_side_effects=True, vmem_limit_bytes=53 * 1024 * 1024
        ),
    )(
        hidden,
        weight,
        momentum,
        gradient,
        jnp.swapaxes(indices, 1, 2),
        counts,
        basis,
    )
    return keys, update, new_momentum


finest_numeric_accuracy = lax.Precision.HIGHEST


def dct_table(length):
    wave_number = jnp.arange(length, dtype=jnp.float32)[:, None]
    position = jnp.arange(length, dtype=jnp.float32)[None, :]
    dct_rows = jnp.cos(jnp.pi * (2.0 * position + 1.0) * wave_number / (2.0 * length)) * jnp.sqrt(
        2.0 / length
    )
    return jnp.where(wave_number == 0.0, dct_rows * jnp.sqrt(0.5), dct_rows)


def make_pair(dct_rows):
    empty_square_tile = jnp.zeros_like(dct_rows)
    upper_half = jnp.concatenate([dct_rows, empty_square_tile], axis=1)
    lower_half = jnp.concatenate([empty_square_tile, dct_rows], axis=1)
    return jnp.concatenate([upper_half, lower_half], axis=0)


def to_spectrum(tile_data, row_basis_operator, paired_cosine_matrix):
    partial_transform = jnp.einsum(
        "ka,tab->tkb", row_basis_operator, tile_data, precision=finest_numeric_accuracy
    )
    return jnp.einsum(
        "tkb,cb->tkc", partial_transform, paired_cosine_matrix, precision=finest_numeric_accuracy
    )


def from_spectrum(tile_frequency_coefficients, row_basis_operator, paired_cosine_matrix):
    partial_transform = jnp.einsum(
        "yh,kyi->khi",
        row_basis_operator,
        tile_frequency_coefficients,
        precision=finest_numeric_accuracy,
    )
    return jnp.einsum(
        "pln,ns->pls", partial_transform, paired_cosine_matrix, precision=finest_numeric_accuracy
    )


def plain(hidden, weight, momentum, gradient, indices, counts):
    tiles_dev, block_side, tile_cols = weight.shape
    kept_count = indices.shape[2]
    replicas = lax.axis_size("rep")
    group_size = lax.axis_size("fsdp")
    all_tiles = tiles_dev * group_size
    width = hidden.shape[1]
    dct_rows = dct_table(block_side)
    paired_cosine_matrix = make_pair(dct_rows)
    moment = decay_rate * momentum[0] + gradient[0].astype(jnp.float32)
    tile_frequency_coefficients = to_spectrum(moment, dct_rows, paired_cosine_matrix)
    span_ids = jnp.arange(2 * tiles_dev, dtype=jnp.int32)[:, None]
    places = (
        span_ids // 2 * (block_side * tile_cols)
        + indices[0] // block_side * tile_cols
        + span_ids % 2 * block_side
        + indices[0] % block_side
    )
    picked = tile_frequency_coefficients.reshape(-1)[places]
    is_live = jnp.arange(kept_count, dtype=jnp.int32)[None, :] < counts[0][:, None]
    kept_values = jnp.where(is_live, picked, jnp.zeros_like(picked))
    flat_size = tiles_dev * block_side * tile_cols
    own_spectra = (
        jnp.zeros((flat_size,), jnp.float32).at[places.reshape(-1)].add(kept_values.reshape(-1))
    )
    own_spectra = own_spectra.reshape(tiles_dev, block_side, tile_cols)
    new_momentum = (moment - from_spectrum(own_spectra, dct_rows, paired_cosine_matrix))[None]
    all_places, all_values = (
        lax.all_gather(places[None], "rep", axis=0, tiled=True),
        lax.all_gather(kept_values[None], "rep", axis=0, tiled=True),
    )
    shared = (
        jnp.zeros((flat_size,), jnp.float32).at[all_places.reshape(-1)].add(all_values.reshape(-1))
    )
    shared = shared.reshape(tiles_dev, block_side, tile_cols) / replicas
    energy = jnp.sum((shared * shared).reshape(tiles_dev, block_side, 2, block_side), axis=(1, 3))
    span_scale = jnp.sqrt(energy / (block_side * block_side) + tiny_eps)
    span_scale = jnp.repeat(span_scale, block_side, axis=1)[:, None, :]
    rows_rep = block_side // replicas
    row_first = lax.axis_index("rep") * rows_rep
    raw_descent_direction = from_spectrum(shared, dct_rows, paired_cosine_matrix)
    update = jnp.tanh(raw_descent_direction / span_scale).astype(jnp.bfloat16)
    revised_parameters = (
        weight.astype(jnp.float32) - step_size * update.astype(jnp.float32)
    ).astype(jnp.bfloat16)
    assembled = lax.all_gather(revised_parameters, "fsdp", axis=0, tiled=True)
    out_update = lax.dynamic_slice_in_dim(update, row_first, rows_rep, 1)
    out_blocks = all_tiles // (width // block_side)
    matrix = assembled.reshape(out_blocks, width // block_side, block_side, tile_cols).transpose(
        1, 2, 0, 3
    )
    matrix = matrix.reshape(width, out_blocks * tile_cols)
    key_states = jnp.dot(hidden, matrix, preferred_element_type=jnp.float32).astype(jnp.bfloat16)
    return (key_states, out_update, new_momentum)


def solution(mesh):
    in_specs = (
        P(("rep", "fsdp"), None),
        P("fsdp", None, None),
        P("rep", "fsdp", None, None),
        P("rep", "fsdp", None, None),
        P("rep", "fsdp", None),
        P("rep", "fsdp"),
    )
    out_specs = (P(("rep", "fsdp"), None), P("fsdp", "rep", None), P("rep", "fsdp", None, None))
    small = mesh.shape["rep"] == 2 and mesh.shape["fsdp"] == 16
    shards = fused if small else plain
    return jax.shard_map(shards, mesh=mesh, in_specs=in_specs, out_specs=out_specs, check_vma=False)
```

```python
import functools

import jax
import jax.numpy as jnp
import numpy as np
from jax import lax
from jax.experimental import pallas as pl
from jax.experimental.pallas import tpu as pltpu
from jax.sharding import PartitionSpec as P

decay_rate = 0.999
step_size = 0.01
tiny_eps = 1e-06
exact = lax.Precision.HIGHEST
MESH = pl.DeviceIdType.MESH
CHUNKS = 10
Z_CHUNKS = 8
X_CHUNKS = 6


def cosine_table(length):
    wave = np.arange(length, dtype=np.float64)[:, None]
    place = np.arange(length, dtype=np.float64)[None, :]
    table = np.cos(np.pi * (2.0 * place + 1.0) * wave / (2.0 * length)) * np.sqrt(2.0 / length)
    return np.where(wave == 0.0, table * np.sqrt(0.5), table)


def split(value):
    high = value.astype(jnp.bfloat16)
    return high, (value - high.astype(jnp.float32)).astype(jnp.bfloat16)


def dot(a, b):
    return jnp.dot(a, b, preferred_element_type=jnp.float32)


def dot_nt(a, b):
    return lax.dot_general(a, b, (((1,), (1,)), ((), ())), preferred_element_type=jnp.float32)


def split3(value):
    high = value.astype(jnp.bfloat16)
    rest = value - high.astype(jnp.float32)
    middle = rest.astype(jnp.bfloat16)
    return high, middle, (rest - middle.astype(jnp.float32)).astype(jnp.bfloat16)


def fused_kernel(
    hidden,
    weight_hbm,
    momentum_hbm,
    gradient_hbm,
    indices,
    counts,
    basis_hbm,
    keys,
    update,
    new_momentum,
    blocks,
    tokens,
    total,
    partial,
    spectra,
    kept,
    kept_other,
    index_other,
    index,
    weight,
    momentum,
    gradient,
    basis,
    raw_index,
    raw_count,
    spread,
    load_sem,
    recv_sem,
    z_sem,
    x_sem,
    y_sem,
    small_send,
    small_recv,
    kept_send,
    kept_recv,
    part_send,
    part_recv,
):
    loads = [
        pltpu.make_async_copy(src, dst, load_sem.at[n])
        for n, (src, dst) in enumerate(
            (
                (indices.at[0], raw_index),
                (counts, raw_count),
                (basis_hbm, basis),
                (momentum_hbm.at[0], momentum),
                (gradient_hbm.at[0], gradient),
                (weight_hbm, weight),
            )
        )
    ]
    for load in loads:
        load.start()
    tiles, side, cols = weight.shape
    per = tiles // CHUNKS
    rows = per * side
    half = tiles * side
    own_tokens = hidden.shape[0]
    pair = 2 * side
    four = 4 * side
    wide = cols * rows // four

    r = lax.axis_index("rep")
    f = lax.axis_index("fsdp")
    z, x, c = f // 4, (f // 2) % 2, f % 2
    middle = jnp.logical_and(z > 0, z < 3)
    up_ok, down_ok = z < 3, z > 0
    y_dev = (1 - r, f)
    x_dev = (r, z * 4 + (1 - x) * 2 + c)
    sib_dev = (r, z * 4 + x * 2 + (1 - c))
    up_dev = (r, jnp.minimum(f + 4, 15 - 3 + f % 4))
    down_dev = (r, jnp.maximum(f - 4, f % 4))

    barrier = pltpu.get_barrier_semaphore()
    for device in (y_dev, x_dev, sib_dev):
        pl.semaphore_signal(barrier, inc=1, device_id=device, device_id_type=MESH)

    @pl.when(up_ok)
    def _():
        pl.semaphore_signal(barrier, inc=1, device_id=up_dev, device_id_type=MESH)

    @pl.when(down_ok)
    def _():
        pl.semaphore_signal(barrier, inc=1, device_id=down_dev, device_id_type=MESH)

    pl.semaphore_wait(barrier, jnp.where(middle, 5, 4))

    def remote(src, dst, send, recv, device):
        return pltpu.make_async_remote_copy(
            src_ref=src, dst_ref=dst, send_sem=send, recv_sem=recv, device_id=device, device_id_type=MESH
        )

    token_copy = remote(
        hidden.at[:, pl.ds(pl.multiple_of((1 - c) * half, 128), half)],
        tokens.at[pl.ds(own_tokens, own_tokens)],
        small_send.at[1],
        small_recv.at[1],
        sib_dev,
    )
    token_local = pltpu.make_async_copy(
        hidden.at[:, pl.ds(pl.multiple_of(c * half, 128), half)],
        tokens.at[pl.ds(0, own_tokens)],
        small_send.at[3],
    )

    def place(p):
        return jnp.where(r == 0, p, CHUNKS - 1 - p)

    def layer(j):
        if j == 0:
            return z
        at_end = jnp.where(z == 0, j, 3 - j)
        flip = (1, 3, 2)[j - 1]
        bits = z // 2, z % 2
        inner = ((bits[0] + flip // 2) % 2) * 2 + (bits[1] + flip % 2) % 2
        return jnp.where(middle, inner, at_end)

    def chunk(o, p):
        q = place(p)
        ref = blocks.at[o, pl.ds(pl.multiple_of(q * rows, rows), rows)]
        return ref, o * CHUNKS + q

    def move(o, p, sems, device):
        ref, n = chunk(o, p)
        return remote(ref, ref, sems.at[n], recv_sem.at[n], device)

    def z_move(o, p, way):
        return move(o, p, z_sem.at[way], up_dev if way == 0 else down_dev)

    lane = lax.broadcasted_iota(jnp.int32, (1, cols), 1)
    row_iota = lax.broadcasted_iota(jnp.int32, (side, cols), 0)
    col_iota = lax.broadcasted_iota(jnp.int32, (cols, cols), 0)
    left_lanes = lane < side
    second = jnp.where(lane % side >= side // 2, side, 0)

    def hot_rows(idx):
        return row_iota == (idx >> 6)

    def hot_cols(idx):
        return (col_iota == ((idx & (side - 1)) + second)).astype(jnp.bfloat16)

    def both_halves(value):
        return value if rows == four else jnp.concatenate([value[:four], value[four:]], axis=1)

    def stacked(value):
        return value if rows == four else jnp.concatenate([value[:, :cols], value[:, cols:]], axis=0)

    def inverse(coefficients):
        one, two = split(both_halves(coefficients))
        right = [basis[n, :wide, :wide] for n in (0, 1)]
        part = dot(one, right[0]) + (dot(one, right[1]) + dot(two, right[0]))
        one, two = split(part)
        return stacked(dot(basis[3], one) + (dot(basis[3], two) + dot(basis[4], one)))

    def transform(value):
        one, two, three = split3(both_halves(value))
        right = [basis[n, :wide, :wide] for n in (3, 4, 5)]
        part = dot(one, right[0]) + (
            (dot(one, right[1]) + dot(two, right[0]))
            + (dot(one, right[2]) + dot(two, right[1]) + dot(three, right[0]))
        )
        one, two, three = split3(part)
        return stacked(
            dot(basis[0], one)
            + (
                (dot(basis[0], two) + dot(basis[1], one))
                + (dot(basis[0], three) + dot(basis[1], two) + dot(basis[2], one))
            )
        )

    def tile_slice(q):
        return pl.ds(q * per if isinstance(q, int) else pl.multiple_of(q * per, per), per)

    def row_slice(q):
        return pl.ds(q * rows if isinstance(q, int) else pl.multiple_of(q * rows, rows), rows)

    def kept_copy(q):
        return remote(kept.at[q], kept_other.at[q], kept_send.at[q], kept_recv.at[q], y_dev)

    def forward(q):
        here = tile_slice(q)
        moment = decay_rate * momentum[here] + gradient[here].astype(jnp.float32)
        new_momentum[0, here] = moment
        spectrum = transform(moment.reshape(rows, cols))
        spectra[row_slice(q)] = spectrum
        idx = index[q]
        found = []
        for t in range(per):
            one = idx[t : t + 1]
            high, low = split(spectrum[t * side : (t + 1) * side])
            taken = dot(jnp.concatenate([high, low], axis=0), hot_cols(one))
            taken = taken[:side] + taken[side:]
            found.append(jnp.sum(jnp.where(hot_rows(one), taken, 0.0), axis=0, keepdims=True))
        kept[q, :per] = jnp.concatenate(found, axis=0)
        kept_copy(q).start()

    own_block = 2 * z + x

    def step(p):
        q = place(p)
        here = tile_slice(q)
        kept_copy(q).wait_recv()
        idx = jnp.where(left_lanes, index[q], index_other[q])
        values = jnp.where(left_lanes, kept[q], kept_other[q]) * 0.5
        dense = []
        for t in range(per):
            one = idx[t : t + 1]
            high, low = split(jnp.where(hot_rows(one), values[t : t + 1], 0.0))
            put = dot_nt(jnp.concatenate([high, low], axis=0), hot_cols(one))
            tile = put[:side] + put[side:]
            energy = jnp.sum(tile * tile, axis=0, keepdims=True)
            left = jnp.sum(jnp.where(left_lanes, energy, 0.0), axis=1, keepdims=True)
            right = jnp.sum(jnp.where(left_lanes, 0.0, energy), axis=1, keepdims=True)
            energy = jnp.where(left_lanes, left, right)
            dense.append(tile * lax.rsqrt(energy / (side * side) + tiny_eps))
        raw = inverse(jnp.concatenate(dense, axis=0))
        direction = jnp.tanh(raw).astype(jnp.bfloat16).astype(jnp.float32)
        tiled = direction.reshape(per, side, cols)
        shown = jnp.where(r == 0, tiled[:, : side // 2], tiled[:, side // 2 :])
        update[here] = shown.astype(jnp.bfloat16)
        old = weight[here].astype(jnp.float32).reshape(rows, cols)
        blocks[own_block, row_slice(q)] = (old - step_size * direction).astype(jnp.bfloat16)

        if p < Z_CHUNKS:

            @pl.when(up_ok)
            def _():
                z_move(own_block, p, 0).start()

            @pl.when(down_ok)
            def _():
                z_move(own_block, p, 1).start()

        if p < X_CHUNKS:
            move(own_block, p, x_sem, x_dev).start()

    def arrived(o, p):
        move(o, p, x_sem, x_dev).wait_recv()

    def from_z(level, p):
        o = 2 * level + x
        arrived(o, p)
        below = level < z

        @pl.when(jnp.logical_and(below, up_ok))
        def _():
            z_move(o, p, 0).start()

        @pl.when(jnp.logical_and(jnp.logical_not(below), down_ok))
        def _():
            z_move(o, p, 1).start()

        if p < X_CHUNKS:
            move(o, p, x_sem, x_dev).start()
        if p < CHUNKS - Z_CHUNKS:
            move(o, p, y_sem, y_dev).start()

    def from_x(j, p):
        o = 2 * layer(j) + (1 - x)
        arrived(o, p)
        if p < CHUNKS - X_CHUNKS:
            move(o, p, y_sem, y_dev).start()

    def settle(q):
        here = tile_slice(q)
        idx = index[q]
        spectrum = spectra[row_slice(q)]
        masks = []
        for t in range(per):
            one = idx[t : t + 1]
            hot = jnp.where(jnp.logical_and(hot_rows(one), left_lanes), 1.0, 0.0).astype(jnp.bfloat16)
            masks.append(dot_nt(hot, hot_cols(one)))
        own = jnp.where(jnp.concatenate(masks, axis=0) > 0.5, spectrum, 0.0)
        new_momentum[0, here] = new_momentum[0, here] - inverse(own).reshape(per, side, cols)

    def near(p):
        from_z(layer(1), p)

        @pl.when(middle)
        def _():
            from_z(layer(2), p)

    def far(p):
        from_z(jnp.where(middle, layer(3), layer(2)), p)

    def farthest(p):
        @pl.when(jnp.logical_not(middle))
        def _():
            from_z(layer(3), p)

    loads[0].wait()
    loads[1].wait()
    listed = raw_index[...]
    position = lax.broadcasted_iota(jnp.int32, listed.shape, 0)
    spread[...] = jnp.full(spread.shape, -1, jnp.int32)
    spread[: listed.shape[0], : listed.shape[1]] = jnp.where(position < raw_count[...], listed, -1)
    spread[...] = jnp.transpose(jnp.concatenate([spread[: listed.shape[0]]] * 4, axis=0))
    joined = jnp.where(
        second > 0, spread[pl.ds(1, tiles, stride=2)], spread[pl.ds(0, tiles, stride=2)]
    )
    index[...] = jnp.full(index.shape, -1, jnp.int32)
    kept[...] = jnp.zeros(kept.shape, jnp.float32)
    for q in range(CHUNKS):
        index[q, :per] = joined[q * per : (q + 1) * per]
    index_copy = remote(index, index_other, small_send.at[0], small_recv.at[0], y_dev)
    index_copy.start()
    for load in loads[2:5]:
        load.wait()
    forward(0)
    token_local.start()
    token_copy.start()
    last = CHUNKS - 1
    forward(last)
    loads[5].wait()
    forward(1)
    forward(last - 1)
    index_copy.wait_recv()
    step(0)
    forward(2)
    forward(last - 2)
    step(1)
    forward(3)
    forward(last - 3)
    step(2)
    near(0)
    from_x(0, 0)
    forward(4)
    forward(last - 4)
    step(3)
    near(1)
    from_x(0, 1)
    for p in range(2, Z_CHUNKS):
        if p + 2 < Z_CHUNKS:
            step(p + 2)
        near(p)
        if p < X_CHUNKS:
            from_x(0, p)

    token_local.wait()
    token_copy.wait_recv()

    def part_copy(j):
        return remote(
            total.at[j, pl.ds(own_tokens, own_tokens)], partial.at[j], part_send.at[j], part_recv.at[j], sib_dev
        )

    def multiply(j):
        o = 2 * layer(j)

        def product(k):
            deep = pl.ds(k * 2 * rows if isinstance(k, int) else pl.multiple_of(k * 2 * rows, 2 * rows), 2 * rows)
            both = jnp.concatenate([blocks[o, deep], blocks[o + 1, deep]], axis=1)
            return dot(tokens[:, deep], both)

        total[j] = product(0)

        def add(k, carry):
            total[j] += product(k)
            return carry

        lax.fori_loop(1, CHUNKS // 2, add, 0)
        part_copy(j).start()

    def rest(j):
        if j > 0:
            for p in range(Z_CHUNKS, CHUNKS):
                arrived(2 * layer(j) + x, p)
        for p in range(X_CHUNKS, CHUNKS):
            arrived(2 * layer(j) + (1 - x), p)
        multiply(j)

    work = [functools.partial(step, p) for p in range(Z_CHUNKS, CHUNKS)]
    work.append(functools.partial(rest, 0))
    work += [functools.partial(settle, q) for q in range(5)]
    work.append(functools.partial(rest, 1))
    work += [functools.partial(settle, q) for q in range(5, CHUNKS)]
    for arrival, j in ((far, 1), (farthest, 2)):
        for p in range(Z_CHUNKS):
            arrival(p)
            if p < X_CHUNKS:
                from_x(j, p)
            if work:
                work.pop(0)()
    for one in work:
        one()
    rest(2)
    for p in range(X_CHUNKS):
        from_x(3, p)
    rest(3)

    for j in range(4):
        part_copy(j).wait_recv()
        columns = pl.ds(pl.multiple_of(layer(j) * 2 * cols, 2 * cols), 2 * cols)
        keys[:, columns] = (total[j, :own_tokens] + partial[j]).astype(jnp.bfloat16)

    index_copy.wait_send()
    token_copy.wait_send()
    for q in range(CHUNKS):
        kept_copy(q).wait_send()
    for j in range(4):
        part_copy(j).wait_send()
        o = 2 * layer(j) + x
        below = layer(j) < z
        above = layer(j) > z
        goes_up = jnp.logical_and(jnp.logical_not(above), up_ok)
        goes_down = jnp.logical_and(jnp.logical_not(below), down_ok)
        for p in range(Z_CHUNKS):

            @pl.when(goes_up)
            def _():
                z_move(o, p, 0).wait_send()

            @pl.when(goes_down)
            def _():
                z_move(o, p, 1).wait_send()

            if p < X_CHUNKS:
                move(o, p, x_sem, x_dev).wait_send()
        if j > 0:
            for p in range(CHUNKS - Z_CHUNKS):
                move(o, p, y_sem, y_dev).wait_send()
        for p in range(CHUNKS - X_CHUNKS):
            move(2 * layer(j) + (1 - x), p, y_sem, y_dev).wait_send()


def fused(hidden, weight, momentum, gradient, indices, counts):
    tiles, side, cols = weight.shape
    kept_count = indices.shape[2]
    half = tiles * side
    own_tokens = hidden.shape[0]
    table = np.kron(np.eye(4), cosine_table(side))
    parts = []
    for rest in (table, table.T):
        for _ in range(3):
            parts.append(rest.astype(jnp.bfloat16))
            rest = rest - parts[-1].astype(np.float64)
    basis = jnp.asarray(np.stack(parts))
    vmem = pl.BlockSpec(memory_space=pltpu.VMEM)
    number = 8 * CHUNKS
    dma = pltpu.SemaphoreType.DMA
    keys, update, new_momentum = pl.pallas_call(
        fused_kernel,
        out_shape=(
            jax.ShapeDtypeStruct((own_tokens, 8 * cols), jnp.bfloat16),
            jax.ShapeDtypeStruct((tiles, side // 2, cols), jnp.bfloat16),
            jax.ShapeDtypeStruct(momentum.shape, jnp.float32),
        ),
        in_specs=[pl.BlockSpec(memory_space=pltpu.HBM)] * 7,
        out_specs=(vmem, vmem, vmem),
        scratch_shapes=[
            pltpu.VMEM((8, half, cols), jnp.bfloat16),
            pltpu.VMEM((2 * own_tokens, half), jnp.bfloat16),
            pltpu.VMEM((4, 2 * own_tokens, 2 * cols), jnp.float32),
            pltpu.VMEM((4, own_tokens, 2 * cols), jnp.float32),
            pltpu.VMEM((half, cols), jnp.float32),
            pltpu.VMEM((CHUNKS, 8, cols), jnp.float32),
            pltpu.VMEM((CHUNKS, 8, cols), jnp.float32),
            pltpu.VMEM((CHUNKS, 8, cols), jnp.int32),
            pltpu.VMEM((CHUNKS, 8, cols), jnp.int32),
            pltpu.VMEM(weight.shape, weight.dtype),
            pltpu.VMEM(momentum.shape[1:], momentum.dtype),
            pltpu.VMEM(gradient.shape[1:], gradient.dtype),
            pltpu.VMEM(basis.shape, basis.dtype),
            pltpu.VMEM((kept_count, 2 * tiles), indices.dtype),
            pltpu.VMEM(counts.shape, counts.dtype),
            pltpu.VMEM((cols, cols), jnp.int32),
            dma((6,)),
            dma((number,)),
            dma((2, number)),
            dma((number,)),
            dma((number,)),
            dma((4,)),
            dma((3,)),
            dma((CHUNKS,)),
            dma((CHUNKS,)),
            dma((4,)),
            dma((4,)),
        ],
        compiler_params=pltpu.CompilerParams(
            collective_id=0, has_side_effects=True, vmem_limit_bytes=53 * 1024 * 1024
        ),
    )(
        hidden,
        weight,
        momentum,
        gradient,
        jnp.swapaxes(indices, 1, 2),
        counts,
        basis,
    )
    return keys, update, new_momentum


finest_numeric_accuracy = lax.Precision.HIGHEST


def dct_table(length):
    wave_number = jnp.arange(length, dtype=jnp.float32)[:, None]
    position = jnp.arange(length, dtype=jnp.float32)[None, :]
    dct_rows = jnp.cos(jnp.pi * (2.0 * position + 1.0) * wave_number / (2.0 * length)) * jnp.sqrt(
        2.0 / length
    )
    return jnp.where(wave_number == 0.0, dct_rows * jnp.sqrt(0.5), dct_rows)


def make_pair(dct_rows):
    empty_square_tile = jnp.zeros_like(dct_rows)
    upper_half = jnp.concatenate([dct_rows, empty_square_tile], axis=1)
    lower_half = jnp.concatenate([empty_square_tile, dct_rows], axis=1)
    return jnp.concatenate([upper_half, lower_half], axis=0)


def to_spectrum(tile_data, row_basis_operator, paired_cosine_matrix):
    partial_transform = jnp.einsum(
        "ka,tab->tkb", row_basis_operator, tile_data, precision=finest_numeric_accuracy
    )
    return jnp.einsum(
        "tkb,cb->tkc", partial_transform, paired_cosine_matrix, precision=finest_numeric_accuracy
    )


def from_spectrum(tile_frequency_coefficients, row_basis_operator, paired_cosine_matrix):
    partial_transform = jnp.einsum(
        "yh,kyi->khi",
        row_basis_operator,
        tile_frequency_coefficients,
        precision=finest_numeric_accuracy,
    )
    return jnp.einsum(
        "pln,ns->pls", partial_transform, paired_cosine_matrix, precision=finest_numeric_accuracy
    )


def plain(hidden, weight, momentum, gradient, indices, counts):
    tiles_dev, block_side, tile_cols = weight.shape
    kept_count = indices.shape[2]
    replicas = lax.axis_size("rep")
    group_size = lax.axis_size("fsdp")
    all_tiles = tiles_dev * group_size
    width = hidden.shape[1]
    dct_rows = dct_table(block_side)
    paired_cosine_matrix = make_pair(dct_rows)
    moment = decay_rate * momentum[0] + gradient[0].astype(jnp.float32)
    tile_frequency_coefficients = to_spectrum(moment, dct_rows, paired_cosine_matrix)
    span_ids = jnp.arange(2 * tiles_dev, dtype=jnp.int32)[:, None]
    places = (
        span_ids // 2 * (block_side * tile_cols)
        + indices[0] // block_side * tile_cols
        + span_ids % 2 * block_side
        + indices[0] % block_side
    )
    picked = tile_frequency_coefficients.reshape(-1)[places]
    is_live = jnp.arange(kept_count, dtype=jnp.int32)[None, :] < counts[0][:, None]
    kept_values = jnp.where(is_live, picked, jnp.zeros_like(picked))
    flat_size = tiles_dev * block_side * tile_cols
    own_spectra = (
        jnp.zeros((flat_size,), jnp.float32).at[places.reshape(-1)].add(kept_values.reshape(-1))
    )
    own_spectra = own_spectra.reshape(tiles_dev, block_side, tile_cols)
    new_momentum = (moment - from_spectrum(own_spectra, dct_rows, paired_cosine_matrix))[None]
    all_places, all_values = (
        lax.all_gather(places[None], "rep", axis=0, tiled=True),
        lax.all_gather(kept_values[None], "rep", axis=0, tiled=True),
    )
    shared = (
        jnp.zeros((flat_size,), jnp.float32).at[all_places.reshape(-1)].add(all_values.reshape(-1))
    )
    shared = shared.reshape(tiles_dev, block_side, tile_cols) / replicas
    energy = jnp.sum((shared * shared).reshape(tiles_dev, block_side, 2, block_side), axis=(1, 3))
    span_scale = jnp.sqrt(energy / (block_side * block_side) + tiny_eps)
    span_scale = jnp.repeat(span_scale, block_side, axis=1)[:, None, :]
    rows_rep = block_side // replicas
    row_first = lax.axis_index("rep") * rows_rep
    raw_descent_direction = from_spectrum(shared, dct_rows, paired_cosine_matrix)
    update = jnp.tanh(raw_descent_direction / span_scale).astype(jnp.bfloat16)
    revised_parameters = (
        weight.astype(jnp.float32) - step_size * update.astype(jnp.float32)
    ).astype(jnp.bfloat16)
    assembled = lax.all_gather(revised_parameters, "fsdp", axis=0, tiled=True)
    out_update = lax.dynamic_slice_in_dim(update, row_first, rows_rep, 1)
    out_blocks = all_tiles // (width // block_side)
    matrix = assembled.reshape(out_blocks, width // block_side, block_side, tile_cols).transpose(
        1, 2, 0, 3
    )
    matrix = matrix.reshape(width, out_blocks * tile_cols)
    key_states = jnp.dot(hidden, matrix, preferred_element_type=jnp.float32).astype(jnp.bfloat16)
    return (key_states, out_update, new_momentum)


def solution(mesh):
    in_specs = (
        P(("rep", "fsdp"), None),
        P("fsdp", None, None),
        P("rep", "fsdp", None, None),
        P("rep", "fsdp", None, None),
        P("rep", "fsdp", None),
        P("rep", "fsdp"),
    )
    out_specs = (P(("rep", "fsdp"), None), P("fsdp", "rep", None), P("rep", "fsdp", None, None))
    small = mesh.shape["rep"] == 2 and mesh.shape["fsdp"] == 16
    shards = fused if small else plain
    return jax.shard_map(shards, mesh=mesh, in_specs=in_specs, out_specs=out_specs, check_vma=False)
```

```python
import functools

import jax
import jax.numpy as jnp
import numpy as np
from jax import lax
from jax.experimental import pallas as pl
from jax.experimental.pallas import tpu as pltpu
from jax.sharding import PartitionSpec as P

decay_rate = 0.999
step_size = 0.01
tiny_eps = 1e-06
exact = lax.Precision.HIGHEST
MESH = pl.DeviceIdType.MESH
CHUNKS = 10
Z_CHUNKS = 8
X_CHUNKS = 6


def cosine_table(length):
    wave = np.arange(length, dtype=np.float64)[:, None]
    place = np.arange(length, dtype=np.float64)[None, :]
    table = np.cos(np.pi * (2.0 * place + 1.0) * wave / (2.0 * length)) * np.sqrt(2.0 / length)
    return np.where(wave == 0.0, table * np.sqrt(0.5), table)


def split(value):
    high = value.astype(jnp.bfloat16)
    return high, (value - high.astype(jnp.float32)).astype(jnp.bfloat16)


def dot(a, b):
    return jnp.dot(a, b, preferred_element_type=jnp.float32)


def dot_nt(a, b):
    return lax.dot_general(a, b, (((1,), (1,)), ((), ())), preferred_element_type=jnp.float32)


def fused_kernel(
    hidden,
    weight_hbm,
    momentum_hbm,
    gradient_hbm,
    indices,
    basis_hbm,
    keys,
    update,
    new_momentum,
    blocks,
    tokens,
    total,
    partial,
    spectra,
    kept,
    kept_other,
    index_other,
    index,
    weight,
    momentum,
    gradient,
    basis,
    raw_index,
    spread,
    load_sem,
    recv_sem,
    z_sem,
    x_sem,
    y_sem,
    small_send,
    small_recv,
    kept_send,
    kept_recv,
    part_send,
    part_recv,
):
    loads = [
        pltpu.make_async_copy(src, dst, load_sem.at[n])
        for n, (src, dst) in enumerate(
            (
                (indices.at[0], raw_index),
                (basis_hbm, basis),
                (momentum_hbm.at[0], momentum),
                (gradient_hbm.at[0], gradient),
                (weight_hbm, weight),
            )
        )
    ]
    for load in loads:
        load.start()
    tiles, side, cols = weight.shape
    per = tiles // CHUNKS
    rows = per * side
    half = tiles * side
    own_tokens = hidden.shape[0]
    pair = 2 * side
    four = 4 * side
    wide = cols * rows // four

    r = lax.axis_index("rep")
    f = lax.axis_index("fsdp")
    z, x, c = f // 4, (f // 2) % 2, f % 2
    middle = jnp.logical_and(z > 0, z < 3)
    up_ok, down_ok = z < 3, z > 0
    y_dev = (1 - r, f)
    x_dev = (r, z * 4 + (1 - x) * 2 + c)
    sib_dev = (r, z * 4 + x * 2 + (1 - c))
    up_dev = (r, jnp.minimum(f + 4, 15 - 3 + f % 4))
    down_dev = (r, jnp.maximum(f - 4, f % 4))

    barrier = pltpu.get_barrier_semaphore()
    for device in (y_dev, x_dev, sib_dev):
        pl.semaphore_signal(barrier, inc=1, device_id=device, device_id_type=MESH)

    @pl.when(up_ok)
    def _():
        pl.semaphore_signal(barrier, inc=1, device_id=up_dev, device_id_type=MESH)

    @pl.when(down_ok)
    def _():
        pl.semaphore_signal(barrier, inc=1, device_id=down_dev, device_id_type=MESH)

    pl.semaphore_wait(barrier, jnp.where(middle, 5, 4))

    def remote(src, dst, send, recv, device):
        return pltpu.make_async_remote_copy(
            src_ref=src, dst_ref=dst, send_sem=send, recv_sem=recv, device_id=device, device_id_type=MESH
        )

    token_copy = remote(
        hidden.at[:, pl.ds(pl.multiple_of((1 - c) * half, 128), half)],
        tokens.at[pl.ds(own_tokens, own_tokens)],
        small_send.at[1],
        small_recv.at[1],
        sib_dev,
    )
    token_local = pltpu.make_async_copy(
        hidden.at[:, pl.ds(pl.multiple_of(c * half, 128), half)],
        tokens.at[pl.ds(0, own_tokens)],
        small_send.at[3],
    )

    def place(p):
        return jnp.where(r == 0, p, CHUNKS - 1 - p)

    def layer(j):
        if j == 0:
            return z
        at_end = jnp.where(z == 0, j, 3 - j)
        flip = (1, 3, 2)[j - 1]
        bits = z // 2, z % 2
        inner = ((bits[0] + flip // 2) % 2) * 2 + (bits[1] + flip % 2) % 2
        return jnp.where(middle, inner, at_end)

    def chunk(o, p):
        q = place(p)
        ref = blocks.at[o, pl.ds(pl.multiple_of(q * rows, rows), rows)]
        return ref, o * CHUNKS + q

    def move(o, p, sems, device):
        ref, n = chunk(o, p)
        return remote(ref, ref, sems.at[n], recv_sem.at[n], device)

    def z_move(o, p, way):
        return move(o, p, z_sem.at[way], up_dev if way == 0 else down_dev)

    lane = lax.broadcasted_iota(jnp.int32, (1, cols), 1)
    row_iota = lax.broadcasted_iota(jnp.int32, (side, cols), 0)
    col_iota = lax.broadcasted_iota(jnp.int32, (cols, cols), 0)
    left_lanes = lane < side
    second = jnp.where(lane % side >= side // 2, side, 0)

    def hot_rows(idx):
        return row_iota == (idx >> 6)

    def hot_cols(idx):
        return (col_iota == ((idx & (side - 1)) + second)).astype(jnp.bfloat16)

    def both_halves(value):
        return value if rows == four else jnp.concatenate([value[:four], value[four:]], axis=1)

    def stacked(value):
        return value if rows == four else jnp.concatenate([value[:, :cols], value[:, cols:]], axis=0)

    def inverse(coefficients):
        one, two = split(both_halves(coefficients))
        right = [basis[n, :wide, :wide] for n in (0, 1)]
        part = dot(one, right[0]) + (dot(one, right[1]) + dot(two, right[0]))
        one, two = split(part)
        return stacked(dot(basis[2], one) + (dot(basis[2], two) + dot(basis[3], one)))

    def transform(value):
        one, two = split(both_halves(value))
        right = [basis[n, :wide, :wide] for n in (2, 3)]
        part = dot(one, right[0]) + (dot(one, right[1]) + dot(two, right[0]))
        one, two = split(part)
        return stacked(dot(basis[0], one) + (dot(basis[0], two) + dot(basis[1], one)))

    def tile_slice(q):
        return pl.ds(q * per if isinstance(q, int) else pl.multiple_of(q * per, per), per)

    def row_slice(q):
        return pl.ds(q * rows if isinstance(q, int) else pl.multiple_of(q * rows, rows), rows)

    def kept_copy(q):
        return remote(kept.at[q], kept_other.at[q], kept_send.at[q], kept_recv.at[q], y_dev)

    def forward(q):
        here = tile_slice(q)
        moment = decay_rate * momentum[here] + gradient[here].astype(jnp.float32)
        new_momentum[0, here] = moment
        spectrum = transform(moment.reshape(rows, cols))
        spectra[row_slice(q)] = spectrum
        idx = index[q]
        found = []
        for t in range(per):
            one = idx[t : t + 1]
            high, low = split(spectrum[t * side : (t + 1) * side])
            taken = dot(jnp.concatenate([high, low], axis=0), hot_cols(one))
            taken = taken[:side] + taken[side:]
            found.append(jnp.sum(jnp.where(hot_rows(one), taken, 0.0), axis=0, keepdims=True))
        kept[q, :per] = jnp.concatenate(found, axis=0)
        kept_copy(q).start()

    own_block = 2 * z + x

    def step(p):
        q = place(p)
        here = tile_slice(q)
        kept_copy(q).wait_recv()
        idx = jnp.where(left_lanes, index[q], index_other[q])
        values = jnp.where(left_lanes, kept[q], kept_other[q]) * 0.5
        dense = []
        for t in range(per):
            one = idx[t : t + 1]
            high, low = split(jnp.where(hot_rows(one), values[t : t + 1], 0.0))
            put = dot_nt(jnp.concatenate([high, low], axis=0), hot_cols(one))
            tile = put[:side] + put[side:]
            energy = jnp.sum(tile * tile, axis=0, keepdims=True)
            left = jnp.sum(jnp.where(left_lanes, energy, 0.0), axis=1, keepdims=True)
            right = jnp.sum(jnp.where(left_lanes, 0.0, energy), axis=1, keepdims=True)
            energy = jnp.where(left_lanes, left, right)
            dense.append(tile * lax.rsqrt(energy / (side * side) + tiny_eps))
        raw = inverse(jnp.concatenate(dense, axis=0))
        direction = jnp.tanh(raw).astype(jnp.bfloat16).astype(jnp.float32)
        tiled = direction.reshape(per, side, cols)
        shown = jnp.where(r == 0, tiled[:, : side // 2], tiled[:, side // 2 :])
        update[here] = shown.astype(jnp.bfloat16)
        old = weight[here].astype(jnp.float32).reshape(rows, cols)
        blocks[own_block, row_slice(q)] = (old - step_size * direction).astype(jnp.bfloat16)

        if p < Z_CHUNKS:

            @pl.when(up_ok)
            def _():
                z_move(own_block, p, 0).start()

            @pl.when(down_ok)
            def _():
                z_move(own_block, p, 1).start()

        if p < X_CHUNKS:
            move(own_block, p, x_sem, x_dev).start()

    def arrived(o, p):
        move(o, p, x_sem, x_dev).wait_recv()

    def from_z(level, p):
        o = 2 * level + x
        arrived(o, p)
        below = level < z

        @pl.when(jnp.logical_and(below, up_ok))
        def _():
            z_move(o, p, 0).start()

        @pl.when(jnp.logical_and(jnp.logical_not(below), down_ok))
        def _():
            z_move(o, p, 1).start()

        if p < X_CHUNKS:
            move(o, p, x_sem, x_dev).start()
        if p < CHUNKS - Z_CHUNKS:
            move(o, p, y_sem, y_dev).start()

    def from_x(j, p):
        o = 2 * layer(j) + (1 - x)
        arrived(o, p)
        if p < CHUNKS - X_CHUNKS:
            move(o, p, y_sem, y_dev).start()

    def settle(q):
        here = tile_slice(q)
        idx = index[q]
        spectrum = spectra[row_slice(q)]
        masks = []
        for t in range(per):
            one = idx[t : t + 1]
            hot = jnp.where(jnp.logical_and(hot_rows(one), left_lanes), 1.0, 0.0).astype(jnp.bfloat16)
            masks.append(dot_nt(hot, hot_cols(one)))
        own = jnp.where(jnp.concatenate(masks, axis=0) > 0.5, spectrum, 0.0)
        new_momentum[0, here] = new_momentum[0, here] - inverse(own).reshape(per, side, cols)

    def near(p):
        from_z(layer(1), p)

        @pl.when(middle)
        def _():
            from_z(layer(2), p)

    def far(p):
        from_z(jnp.where(middle, layer(3), layer(2)), p)

    def farthest(p):
        @pl.when(jnp.logical_not(middle))
        def _():
            from_z(layer(3), p)

    loads[0].wait()
    listed = raw_index[...]
    spread[...] = jnp.full(spread.shape, -1, jnp.int32)
    spread[: listed.shape[0], : listed.shape[1]] = listed
    spread[...] = jnp.transpose(jnp.concatenate([spread[: listed.shape[0]]] * 4, axis=0))
    joined = jnp.where(
        second > 0, spread[pl.ds(1, tiles, stride=2)], spread[pl.ds(0, tiles, stride=2)]
    )
    index[...] = jnp.full(index.shape, -1, jnp.int32)
    kept[...] = jnp.zeros(kept.shape, jnp.float32)
    for q in range(CHUNKS):
        index[q, :per] = joined[q * per : (q + 1) * per]
    index_copy = remote(index, index_other, small_send.at[0], small_recv.at[0], y_dev)
    index_copy.start()
    for load in loads[1:4]:
        load.wait()
    forward(0)
    token_local.start()
    token_copy.start()
    last = CHUNKS - 1
    forward(last)
    loads[4].wait()
    forward(1)
    forward(last - 1)
    index_copy.wait_recv()
    step(0)
    forward(2)
    forward(last - 2)
    step(1)
    forward(3)
    forward(last - 3)
    step(2)
    near(0)
    from_x(0, 0)
    forward(4)
    forward(last - 4)
    step(3)
    near(1)
    from_x(0, 1)
    for p in range(2, Z_CHUNKS):
        if p + 2 < Z_CHUNKS:
            step(p + 2)
        near(p)
        if p < X_CHUNKS:
            from_x(0, p)

    token_local.wait()
    token_copy.wait_recv()

    def part_copy(j):
        return remote(
            total.at[j, pl.ds(own_tokens, own_tokens)], partial.at[j], part_send.at[j], part_recv.at[j], sib_dev
        )

    def multiply(j):
        o = 2 * layer(j)

        def product(k):
            deep = pl.ds(k * 2 * rows if isinstance(k, int) else pl.multiple_of(k * 2 * rows, 2 * rows), 2 * rows)
            both = jnp.concatenate([blocks[o, deep], blocks[o + 1, deep]], axis=1)
            return dot(tokens[:, deep], both)

        total[j] = product(0)

        def add(k, carry):
            total[j] += product(k)
            return carry

        lax.fori_loop(1, CHUNKS // 2, add, 0)
        part_copy(j).start()

    def rest(j):
        if j > 0:
            for p in range(Z_CHUNKS, CHUNKS):
                arrived(2 * layer(j) + x, p)
        for p in range(X_CHUNKS, CHUNKS):
            arrived(2 * layer(j) + (1 - x), p)
        multiply(j)

    work = [functools.partial(step, p) for p in range(Z_CHUNKS, CHUNKS)]
    work.append(functools.partial(rest, 0))
    work += [functools.partial(settle, q) for q in range(5)]
    work.append(functools.partial(rest, 1))
    work += [functools.partial(settle, q) for q in range(5, CHUNKS)]
    for arrival, j in ((far, 1), (farthest, 2)):
        for p in range(Z_CHUNKS):
            arrival(p)
            if p < X_CHUNKS:
                from_x(j, p)
            if work:
                work.pop(0)()
    for one in work:
        one()
    rest(2)

    def piece(p):
        first = pl.multiple_of(jnp.minimum(place(p), place(p + 1)) * rows, 2 * rows)
        deep = pl.ds(first, 2 * rows)
        o = 2 * layer(3)
        both = jnp.concatenate([blocks[o, deep], blocks[o + 1, deep]], axis=1)
        return dot(tokens[:, deep], both)

    for p in range(CHUNKS - X_CHUNKS):
        from_x(3, p)
    total[3] = piece(0)
    total[3] += piece(2)
    for p in range(CHUNKS - X_CHUNKS, X_CHUNKS):
        from_x(3, p)
    total[3] += piece(4)
    for p in range(Z_CHUNKS, CHUNKS):
        arrived(2 * layer(3) + x, p)
        arrived(2 * layer(3) + (1 - x), p)
    total[3] += piece(8)
    for p in range(X_CHUNKS, Z_CHUNKS):
        arrived(2 * layer(3) + (1 - x), p)
    total[3] += piece(6)
    part_copy(3).start()

    for j in range(4):
        part_copy(j).wait_recv()
        columns = pl.ds(pl.multiple_of(layer(j) * 2 * cols, 2 * cols), 2 * cols)
        keys[:, columns] = (total[j, :own_tokens] + partial[j]).astype(jnp.bfloat16)

    index_copy.wait_send()
    token_copy.wait_send()
    for q in range(CHUNKS):
        kept_copy(q).wait_send()
    for j in range(4):
        part_copy(j).wait_send()
        o = 2 * layer(j) + x
        below = layer(j) < z
        above = layer(j) > z
        goes_up = jnp.logical_and(jnp.logical_not(above), up_ok)
        goes_down = jnp.logical_and(jnp.logical_not(below), down_ok)
        for p in range(Z_CHUNKS):

            @pl.when(goes_up)
            def _():
                z_move(o, p, 0).wait_send()

            @pl.when(goes_down)
            def _():
                z_move(o, p, 1).wait_send()

            if p < X_CHUNKS:
                move(o, p, x_sem, x_dev).wait_send()
        if j > 0:
            for p in range(CHUNKS - Z_CHUNKS):
                move(o, p, y_sem, y_dev).wait_send()
        for p in range(CHUNKS - X_CHUNKS):
            move(2 * layer(j) + (1 - x), p, y_sem, y_dev).wait_send()


def fused(hidden, weight, momentum, gradient, indices, counts):
    tiles, side, cols = weight.shape
    kept_count = indices.shape[2]
    half = tiles * side
    own_tokens = hidden.shape[0]
    live = jnp.arange(kept_count, dtype=jnp.int32)[None, :, None] < counts[:, None, :]
    listed = jnp.where(live, jnp.swapaxes(indices, 1, 2), -1)
    table = np.kron(np.eye(4), cosine_table(side))
    parts = []
    for rest in (table, table.T):
        for _ in range(2):
            parts.append(rest.astype(jnp.bfloat16))
            rest = rest - parts[-1].astype(np.float64)
    basis = jnp.asarray(np.stack(parts))
    vmem = pl.BlockSpec(memory_space=pltpu.VMEM)
    number = 8 * CHUNKS
    dma = pltpu.SemaphoreType.DMA
    keys, update, new_momentum = pl.pallas_call(
        fused_kernel,
        out_shape=(
            jax.ShapeDtypeStruct((own_tokens, 8 * cols), jnp.bfloat16),
            jax.ShapeDtypeStruct((tiles, side // 2, cols), jnp.bfloat16),
            jax.ShapeDtypeStruct(momentum.shape, jnp.float32),
        ),
        in_specs=[pl.BlockSpec(memory_space=pltpu.HBM)] * 6,
        out_specs=(vmem, vmem, vmem),
        scratch_shapes=[
            pltpu.VMEM((8, half, cols), jnp.bfloat16),
            pltpu.VMEM((2 * own_tokens, half), jnp.bfloat16),
            pltpu.VMEM((4, 2 * own_tokens, 2 * cols), jnp.float32),
            pltpu.VMEM((4, own_tokens, 2 * cols), jnp.float32),
            pltpu.VMEM((half, cols), jnp.float32),
            pltpu.VMEM((CHUNKS, 8, cols), jnp.float32),
            pltpu.VMEM((CHUNKS, 8, cols), jnp.float32),
            pltpu.VMEM((CHUNKS, 8, cols), jnp.int32),
            pltpu.VMEM((CHUNKS, 8, cols), jnp.int32),
            pltpu.VMEM(weight.shape, weight.dtype),
            pltpu.VMEM(momentum.shape[1:], momentum.dtype),
            pltpu.VMEM(gradient.shape[1:], gradient.dtype),
            pltpu.VMEM(basis.shape, basis.dtype),
            pltpu.VMEM((kept_count, 2 * tiles), indices.dtype),
            pltpu.VMEM((cols, cols), jnp.int32),
            dma((5,)),
            dma((number,)),
            dma((2, number)),
            dma((number,)),
            dma((number,)),
            dma((4,)),
            dma((3,)),
            dma((CHUNKS,)),
            dma((CHUNKS,)),
            dma((4,)),
            dma((4,)),
        ],
        compiler_params=pltpu.CompilerParams(
            collective_id=0, has_side_effects=True, vmem_limit_bytes=53 * 1024 * 1024
        ),
    )(
        hidden,
        weight,
        momentum,
        gradient,
        listed,
        basis,
    )
    return keys, update, new_momentum


finest_numeric_accuracy = lax.Precision.HIGHEST


def dct_table(length):
    wave_number = jnp.arange(length, dtype=jnp.float32)[:, None]
    position = jnp.arange(length, dtype=jnp.float32)[None, :]
    dct_rows = jnp.cos(jnp.pi * (2.0 * position + 1.0) * wave_number / (2.0 * length)) * jnp.sqrt(
        2.0 / length
    )
    return jnp.where(wave_number == 0.0, dct_rows * jnp.sqrt(0.5), dct_rows)


def make_pair(dct_rows):
    empty_square_tile = jnp.zeros_like(dct_rows)
    upper_half = jnp.concatenate([dct_rows, empty_square_tile], axis=1)
    lower_half = jnp.concatenate([empty_square_tile, dct_rows], axis=1)
    return jnp.concatenate([upper_half, lower_half], axis=0)


def to_spectrum(tile_data, row_basis_operator, paired_cosine_matrix):
    partial_transform = jnp.einsum(
        "ka,tab->tkb", row_basis_operator, tile_data, precision=finest_numeric_accuracy
    )
    return jnp.einsum(
        "tkb,cb->tkc", partial_transform, paired_cosine_matrix, precision=finest_numeric_accuracy
    )


def from_spectrum(tile_frequency_coefficients, row_basis_operator, paired_cosine_matrix):
    partial_transform = jnp.einsum(
        "yh,kyi->khi",
        row_basis_operator,
        tile_frequency_coefficients,
        precision=finest_numeric_accuracy,
    )
    return jnp.einsum(
        "pln,ns->pls", partial_transform, paired_cosine_matrix, precision=finest_numeric_accuracy
    )


def plain(hidden, weight, momentum, gradient, indices, counts):
    tiles_dev, block_side, tile_cols = weight.shape
    kept_count = indices.shape[2]
    replicas = lax.axis_size("rep")
    group_size = lax.axis_size("fsdp")
    all_tiles = tiles_dev * group_size
    width = hidden.shape[1]
    dct_rows = dct_table(block_side)
    paired_cosine_matrix = make_pair(dct_rows)
    moment = decay_rate * momentum[0] + gradient[0].astype(jnp.float32)
    tile_frequency_coefficients = to_spectrum(moment, dct_rows, paired_cosine_matrix)
    span_ids = jnp.arange(2 * tiles_dev, dtype=jnp.int32)[:, None]
    places = (
        span_ids // 2 * (block_side * tile_cols)
        + indices[0] // block_side * tile_cols
        + span_ids % 2 * block_side
        + indices[0] % block_side
    )
    picked = tile_frequency_coefficients.reshape(-1)[places]
    is_live = jnp.arange(kept_count, dtype=jnp.int32)[None, :] < counts[0][:, None]
    kept_values = jnp.where(is_live, picked, jnp.zeros_like(picked))
    flat_size = tiles_dev * block_side * tile_cols
    own_spectra = (
        jnp.zeros((flat_size,), jnp.float32).at[places.reshape(-1)].add(kept_values.reshape(-1))
    )
    own_spectra = own_spectra.reshape(tiles_dev, block_side, tile_cols)
    new_momentum = (moment - from_spectrum(own_spectra, dct_rows, paired_cosine_matrix))[None]
    all_places, all_values = (
        lax.all_gather(places[None], "rep", axis=0, tiled=True),
        lax.all_gather(kept_values[None], "rep", axis=0, tiled=True),
    )
    shared = (
        jnp.zeros((flat_size,), jnp.float32).at[all_places.reshape(-1)].add(all_values.reshape(-1))
    )
    shared = shared.reshape(tiles_dev, block_side, tile_cols) / replicas
    energy = jnp.sum((shared * shared).reshape(tiles_dev, block_side, 2, block_side), axis=(1, 3))
    span_scale = jnp.sqrt(energy / (block_side * block_side) + tiny_eps)
    span_scale = jnp.repeat(span_scale, block_side, axis=1)[:, None, :]
    rows_rep = block_side // replicas
    row_first = lax.axis_index("rep") * rows_rep
    raw_descent_direction = from_spectrum(shared, dct_rows, paired_cosine_matrix)
    update = jnp.tanh(raw_descent_direction / span_scale).astype(jnp.bfloat16)
    revised_parameters = (
        weight.astype(jnp.float32) - step_size * update.astype(jnp.float32)
    ).astype(jnp.bfloat16)
    assembled = lax.all_gather(revised_parameters, "fsdp", axis=0, tiled=True)
    out_update = lax.dynamic_slice_in_dim(update, row_first, rows_rep, 1)
    out_blocks = all_tiles // (width // block_side)
    matrix = assembled.reshape(out_blocks, width // block_side, block_side, tile_cols).transpose(
        1, 2, 0, 3
    )
    matrix = matrix.reshape(width, out_blocks * tile_cols)
    key_states = jnp.dot(hidden, matrix, preferred_element_type=jnp.float32).astype(jnp.bfloat16)
    return (key_states, out_update, new_momentum)


def solution(mesh):
    in_specs = (
        P(("rep", "fsdp"), None),
        P("fsdp", None, None),
        P("rep", "fsdp", None, None),
        P("rep", "fsdp", None, None),
        P("rep", "fsdp", None),
        P("rep", "fsdp"),
    )
    out_specs = (P(("rep", "fsdp"), None), P("fsdp", "rep", None), P("rep", "fsdp", None, None))
    small = mesh.shape["rep"] == 2 and mesh.shape["fsdp"] == 16
    shards = fused if small else plain
    return jax.shard_map(shards, mesh=mesh, in_specs=in_specs, out_specs=out_specs, check_vma=False)
```

```python
import functools

import jax
import jax.numpy as jnp
import numpy as np
from jax import lax
from jax.experimental import pallas as pl
from jax.experimental.pallas import tpu as pltpu
from jax.sharding import PartitionSpec as P

decay_rate = 0.999
step_size = 0.01
tiny_eps = 1e-06
exact = lax.Precision.HIGHEST
MESH = pl.DeviceIdType.MESH
CHUNKS = 10
Z_CHUNKS = 7
X_CHUNKS = 6


def cosine_table(length):
    wave = np.arange(length, dtype=np.float64)[:, None]
    place = np.arange(length, dtype=np.float64)[None, :]
    table = np.cos(np.pi * (2.0 * place + 1.0) * wave / (2.0 * length)) * np.sqrt(2.0 / length)
    return np.where(wave == 0.0, table * np.sqrt(0.5), table)


def split(value):
    high = value.astype(jnp.bfloat16)
    return high, (value - high.astype(jnp.float32)).astype(jnp.bfloat16)


def dot(a, b):
    return jnp.dot(a, b, preferred_element_type=jnp.float32)


def dot_nt(a, b):
    return lax.dot_general(a, b, (((1,), (1,)), ((), ())), preferred_element_type=jnp.float32)


def fused_kernel(
    hidden,
    weight_hbm,
    momentum_hbm,
    gradient_hbm,
    indices,
    basis_hbm,
    keys,
    update,
    new_momentum,
    blocks,
    tokens,
    total,
    partial,
    spectra,
    kept,
    kept_other,
    index_other,
    index,
    weight,
    momentum,
    gradient,
    basis,
    raw_index,
    spread,
    load_sem,
    recv_sem,
    z_sem,
    x_sem,
    y_sem,
    small_send,
    small_recv,
    kept_send,
    kept_recv,
    part_send,
    part_recv,
):
    loads = [
        pltpu.make_async_copy(src, dst, load_sem.at[n])
        for n, (src, dst) in enumerate(
            (
                (indices.at[0], raw_index),
                (basis_hbm, basis),
                (momentum_hbm.at[0], momentum),
                (gradient_hbm.at[0], gradient),
                (weight_hbm, weight),
            )
        )
    ]
    for load in loads:
        load.start()
    tiles, side, cols = weight.shape
    per = tiles // CHUNKS
    rows = per * side
    half = tiles * side
    own_tokens = hidden.shape[0]
    pair = 2 * side
    four = 4 * side
    wide = cols * rows // four

    r = lax.axis_index("rep")
    f = lax.axis_index("fsdp")
    z, x, c = f // 4, (f // 2) % 2, f % 2
    middle = jnp.logical_and(z > 0, z < 3)
    up_ok, down_ok = z < 3, z > 0
    y_dev = (1 - r, f)
    x_dev = (r, z * 4 + (1 - x) * 2 + c)
    sib_dev = (r, z * 4 + x * 2 + (1 - c))
    up_dev = (r, jnp.minimum(f + 4, 15 - 3 + f % 4))
    down_dev = (r, jnp.maximum(f - 4, f % 4))

    barrier = pltpu.get_barrier_semaphore()
    for device in (y_dev, x_dev, sib_dev):
        pl.semaphore_signal(barrier, inc=1, device_id=device, device_id_type=MESH)

    @pl.when(up_ok)
    def _():
        pl.semaphore_signal(barrier, inc=1, device_id=up_dev, device_id_type=MESH)

    @pl.when(down_ok)
    def _():
        pl.semaphore_signal(barrier, inc=1, device_id=down_dev, device_id_type=MESH)

    pl.semaphore_wait(barrier, jnp.where(middle, 5, 4))

    def remote(src, dst, send, recv, device):
        return pltpu.make_async_remote_copy(
            src_ref=src, dst_ref=dst, send_sem=send, recv_sem=recv, device_id=device, device_id_type=MESH
        )

    token_copy = remote(
        hidden.at[:, pl.ds(pl.multiple_of((1 - c) * half, 128), half)],
        tokens.at[pl.ds(own_tokens, own_tokens)],
        small_send.at[1],
        small_recv.at[1],
        sib_dev,
    )
    token_local = pltpu.make_async_copy(
        hidden.at[:, pl.ds(pl.multiple_of(c * half, 128), half)],
        tokens.at[pl.ds(0, own_tokens)],
        small_send.at[3],
    )

    def place(p):
        return jnp.where(r == 0, p, CHUNKS - 1 - p)

    def layer(j):
        if j == 0:
            return z
        at_end = jnp.where(z == 0, j, 3 - j)
        flip = (1, 3, 2)[j - 1]
        bits = z // 2, z % 2
        inner = ((bits[0] + flip // 2) % 2) * 2 + (bits[1] + flip % 2) % 2
        return jnp.where(middle, inner, at_end)

    def chunk(o, p):
        q = place(p)
        ref = blocks.at[o, pl.ds(pl.multiple_of(q * rows, rows), rows)]
        return ref, o * CHUNKS + q

    def move(o, p, sems, device):
        ref, n = chunk(o, p)
        return remote(ref, ref, sems.at[n], recv_sem.at[n], device)

    def z_move(o, p, way):
        return move(o, p, z_sem.at[way], up_dev if way == 0 else down_dev)

    lane = lax.broadcasted_iota(jnp.int32, (1, cols), 1)
    row_iota = lax.broadcasted_iota(jnp.int32, (side, cols), 0)
    col_iota = lax.broadcasted_iota(jnp.int32, (cols, cols), 0)
    left_lanes = lane < side
    second = jnp.where(lane % side >= side // 2, side, 0)

    def hot_rows(idx):
        return row_iota == (idx >> 6)

    def hot_cols(idx):
        return (col_iota == ((idx & (side - 1)) + second)).astype(jnp.bfloat16)

    def both_halves(value):
        return value if rows == four else jnp.concatenate([value[:four], value[four:]], axis=1)

    def stacked(value):
        return value if rows == four else jnp.concatenate([value[:, :cols], value[:, cols:]], axis=0)

    def inverse(coefficients):
        one, two = split(both_halves(coefficients))
        right = [basis[n, :wide, :wide] for n in (0, 1)]
        part = dot(one, right[0]) + (dot(one, right[1]) + dot(two, right[0]))
        one, two = split(part)
        return stacked(dot(basis[2], one) + (dot(basis[2], two) + dot(basis[3], one)))

    def transform(value):
        one, two = split(both_halves(value))
        right = [basis[n, :wide, :wide] for n in (2, 3)]
        part = dot(one, right[0]) + (dot(one, right[1]) + dot(two, right[0]))
        one, two = split(part)
        return stacked(dot(basis[0], one) + (dot(basis[0], two) + dot(basis[1], one)))

    def tile_slice(q):
        return pl.ds(q * per if isinstance(q, int) else pl.multiple_of(q * per, per), per)

    def row_slice(q):
        return pl.ds(q * rows if isinstance(q, int) else pl.multiple_of(q * rows, rows), rows)

    def kept_copy(q):
        return remote(kept.at[q], kept_other.at[q], kept_send.at[q], kept_recv.at[q], y_dev)

    def forward(q):
        here = tile_slice(q)
        moment = decay_rate * momentum[here] + gradient[here].astype(jnp.float32)
        new_momentum[0, here] = moment
        spectrum = transform(moment.reshape(rows, cols))
        spectra[row_slice(q)] = spectrum
        idx = index[q]
        found = []
        for t in range(per):
            one = idx[t : t + 1]
            high, low = split(spectrum[t * side : (t + 1) * side])
            taken = dot(jnp.concatenate([high, low], axis=0), hot_cols(one))
            taken = taken[:side] + taken[side:]
            found.append(jnp.sum(jnp.where(hot_rows(one), taken, 0.0), axis=0, keepdims=True))
        kept[q, :per] = jnp.concatenate(found, axis=0)
        kept_copy(q).start()

    own_block = 2 * z + x

    def step(p):
        q = place(p)
        here = tile_slice(q)
        kept_copy(q).wait_recv()
        idx = jnp.where(left_lanes, index[q], index_other[q])
        values = jnp.where(left_lanes, kept[q], kept_other[q]) * 0.5
        dense = []
        for t in range(per):
            one = idx[t : t + 1]
            high, low = split(jnp.where(hot_rows(one), values[t : t + 1], 0.0))
            put = dot_nt(jnp.concatenate([high, low], axis=0), hot_cols(one))
            tile = put[:side] + put[side:]
            energy = jnp.sum(tile * tile, axis=0, keepdims=True)
            left = jnp.sum(jnp.where(left_lanes, energy, 0.0), axis=1, keepdims=True)
            right = jnp.sum(jnp.where(left_lanes, 0.0, energy), axis=1, keepdims=True)
            energy = jnp.where(left_lanes, left, right)
            dense.append(tile * lax.rsqrt(energy / (side * side) + tiny_eps))
        raw = inverse(jnp.concatenate(dense, axis=0))
        direction = jnp.tanh(raw).astype(jnp.bfloat16).astype(jnp.float32)
        tiled = direction.reshape(per, side, cols)
        shown = jnp.where(r == 0, tiled[:, : side // 2], tiled[:, side // 2 :])
        update[here] = shown.astype(jnp.bfloat16)
        old = weight[here].astype(jnp.float32).reshape(rows, cols)
        blocks[own_block, row_slice(q)] = (old - step_size * direction).astype(jnp.bfloat16)

        if p < Z_CHUNKS:

            @pl.when(up_ok)
            def _():
                z_move(own_block, p, 0).start()

            @pl.when(down_ok)
            def _():
                z_move(own_block, p, 1).start()

        if p < X_CHUNKS:
            move(own_block, p, x_sem, x_dev).start()

    def arrived(o, p):
        move(o, p, x_sem, x_dev).wait_recv()

    def from_z(level, p):
        o = 2 * level + x
        arrived(o, p)
        below = level < z

        @pl.when(jnp.logical_and(below, up_ok))
        def _():
            z_move(o, p, 0).start()

        @pl.when(jnp.logical_and(jnp.logical_not(below), down_ok))
        def _():
            z_move(o, p, 1).start()

        if p < X_CHUNKS:
            move(o, p, x_sem, x_dev).start()
        if p < CHUNKS - Z_CHUNKS:
            move(o, p, y_sem, y_dev).start()

    def from_x(j, p):
        o = 2 * layer(j) + (1 - x)
        arrived(o, p)
        if p < CHUNKS - X_CHUNKS:
            move(o, p, y_sem, y_dev).start()

    def settle(q):
        here = tile_slice(q)
        idx = index[q]
        spectrum = spectra[row_slice(q)]
        masks = []
        for t in range(per):
            one = idx[t : t + 1]
            hot = jnp.where(jnp.logical_and(hot_rows(one), left_lanes), 1.0, 0.0).astype(jnp.bfloat16)
            masks.append(dot_nt(hot, hot_cols(one)))
        own = jnp.where(jnp.concatenate(masks, axis=0) > 0.5, spectrum, 0.0)
        new_momentum[0, here] = new_momentum[0, here] - inverse(own).reshape(per, side, cols)

    def near(p):
        from_z(layer(1), p)

        @pl.when(middle)
        def _():
            from_z(layer(2), p)

    def far(p):
        from_z(jnp.where(middle, layer(3), layer(2)), p)

    def farthest(p):
        @pl.when(jnp.logical_not(middle))
        def _():
            from_z(layer(3), p)

    loads[0].wait()
    listed = raw_index[...]
    spread[...] = jnp.full(spread.shape, -1, jnp.int32)
    spread[: listed.shape[0], : listed.shape[1]] = listed
    spread[...] = jnp.transpose(jnp.concatenate([spread[: listed.shape[0]]] * 4, axis=0))
    joined = jnp.where(
        second > 0, spread[pl.ds(1, tiles, stride=2)], spread[pl.ds(0, tiles, stride=2)]
    )
    index[...] = jnp.full(index.shape, -1, jnp.int32)
    kept[...] = jnp.zeros(kept.shape, jnp.float32)
    for q in range(CHUNKS):
        index[q, :per] = joined[q * per : (q + 1) * per]
    index_copy = remote(index, index_other, small_send.at[0], small_recv.at[0], y_dev)
    index_copy.start()
    for load in loads[1:4]:
        load.wait()
    forward(0)
    token_local.start()
    token_copy.start()
    last = CHUNKS - 1
    forward(last)
    loads[4].wait()
    forward(1)
    forward(last - 1)
    index_copy.wait_recv()
    step(0)
    forward(2)
    forward(last - 2)
    step(1)
    forward(3)
    forward(last - 3)
    step(2)
    near(0)
    from_x(0, 0)
    forward(4)
    forward(last - 4)
    step(3)
    near(1)
    from_x(0, 1)
    for p in range(2, Z_CHUNKS):
        if p + 2 < Z_CHUNKS:
            step(p + 2)
        near(p)
        if p < X_CHUNKS:
            from_x(0, p)

    token_local.wait()
    token_copy.wait_recv()

    def part_copy(j):
        return remote(
            total.at[j, pl.ds(own_tokens, own_tokens)], partial.at[j], part_send.at[j], part_recv.at[j], sib_dev
        )

    def multiply(j):
        o = 2 * layer(j)

        def product(k):
            deep = pl.ds(k * 2 * rows if isinstance(k, int) else pl.multiple_of(k * 2 * rows, 2 * rows), 2 * rows)
            both = jnp.concatenate([blocks[o, deep], blocks[o + 1, deep]], axis=1)
            return dot(tokens[:, deep], both)

        total[j] = product(0)

        def add(k, carry):
            total[j] += product(k)
            return carry

        lax.fori_loop(1, CHUNKS // 2, add, 0)
        part_copy(j).start()

    def rest(j):
        if j > 0:
            for p in range(Z_CHUNKS, CHUNKS):
                arrived(2 * layer(j) + x, p)
        for p in range(X_CHUNKS, CHUNKS):
            arrived(2 * layer(j) + (1 - x), p)
        multiply(j)

    work = [functools.partial(step, p) for p in range(Z_CHUNKS, CHUNKS)]
    work.append(functools.partial(rest, 0))
    work += [functools.partial(settle, q) for q in range(5)]
    work.append(functools.partial(rest, 1))
    work += [functools.partial(settle, q) for q in range(5, CHUNKS)]
    for arrival, j in ((far, 1), (farthest, 2)):
        for p in range(Z_CHUNKS):
            arrival(p)
            if p < X_CHUNKS:
                from_x(j, p)
            if work:
                work.pop(0)()
    for one in work:
        one()
    rest(2)

    def piece(p):
        first = pl.multiple_of(jnp.minimum(place(p), place(p + 1)) * rows, 2 * rows)
        deep = pl.ds(first, 2 * rows)
        o = 2 * layer(3)
        both = jnp.concatenate([blocks[o, deep], blocks[o + 1, deep]], axis=1)
        return dot(tokens[:, deep], both)

    for p in range(CHUNKS - X_CHUNKS):
        from_x(3, p)
    total[3] = piece(0)
    total[3] += piece(2)
    for p in range(CHUNKS - X_CHUNKS, X_CHUNKS):
        from_x(3, p)
    total[3] += piece(4)
    for p in range(Z_CHUNKS, CHUNKS):
        arrived(2 * layer(3) + x, p)
        arrived(2 * layer(3) + (1 - x), p)
    total[3] += piece(8)
    for p in range(X_CHUNKS, Z_CHUNKS):
        arrived(2 * layer(3) + (1 - x), p)
    total[3] += piece(6)
    part_copy(3).start()

    for j in range(4):
        part_copy(j).wait_recv()
        columns = pl.ds(pl.multiple_of(layer(j) * 2 * cols, 2 * cols), 2 * cols)
        keys[:, columns] = (total[j, :own_tokens] + partial[j]).astype(jnp.bfloat16)

    index_copy.wait_send()
    token_copy.wait_send()
    for q in range(CHUNKS):
        kept_copy(q).wait_send()
    for j in range(4):
        part_copy(j).wait_send()
        o = 2 * layer(j) + x
        below = layer(j) < z
        above = layer(j) > z
        goes_up = jnp.logical_and(jnp.logical_not(above), up_ok)
        goes_down = jnp.logical_and(jnp.logical_not(below), down_ok)
        for p in range(Z_CHUNKS):

            @pl.when(goes_up)
            def _():
                z_move(o, p, 0).wait_send()

            @pl.when(goes_down)
            def _():
                z_move(o, p, 1).wait_send()

            if p < X_CHUNKS:
                move(o, p, x_sem, x_dev).wait_send()
        if j > 0:
            for p in range(CHUNKS - Z_CHUNKS):
                move(o, p, y_sem, y_dev).wait_send()
        for p in range(CHUNKS - X_CHUNKS):
            move(2 * layer(j) + (1 - x), p, y_sem, y_dev).wait_send()


def fused(hidden, weight, momentum, gradient, indices, counts):
    tiles, side, cols = weight.shape
    kept_count = indices.shape[2]
    half = tiles * side
    own_tokens = hidden.shape[0]
    live = jnp.arange(kept_count, dtype=jnp.int32)[None, :, None] < counts[:, None, :]
    listed = jnp.where(live, jnp.swapaxes(indices, 1, 2), -1)
    table = np.kron(np.eye(4), cosine_table(side))
    parts = []
    for rest in (table, table.T):
        for _ in range(2):
            parts.append(rest.astype(jnp.bfloat16))
            rest = rest - parts[-1].astype(np.float64)
    basis = jnp.asarray(np.stack(parts))
    vmem = pl.BlockSpec(memory_space=pltpu.VMEM)
    number = 8 * CHUNKS
    dma = pltpu.SemaphoreType.DMA
    keys, update, new_momentum = pl.pallas_call(
        fused_kernel,
        out_shape=(
            jax.ShapeDtypeStruct((own_tokens, 8 * cols), jnp.bfloat16),
            jax.ShapeDtypeStruct((tiles, side // 2, cols), jnp.bfloat16),
            jax.ShapeDtypeStruct(momentum.shape, jnp.float32),
        ),
        in_specs=[pl.BlockSpec(memory_space=pltpu.HBM)] * 6,
        out_specs=(vmem, vmem, vmem),
        scratch_shapes=[
            pltpu.VMEM((8, half, cols), jnp.bfloat16),
            pltpu.VMEM((2 * own_tokens, half), jnp.bfloat16),
            pltpu.VMEM((4, 2 * own_tokens, 2 * cols), jnp.float32),
            pltpu.VMEM((4, own_tokens, 2 * cols), jnp.float32),
            pltpu.VMEM((half, cols), jnp.float32),
            pltpu.VMEM((CHUNKS, 8, cols), jnp.float32),
            pltpu.VMEM((CHUNKS, 8, cols), jnp.float32),
            pltpu.VMEM((CHUNKS, 8, cols), jnp.int32),
            pltpu.VMEM((CHUNKS, 8, cols), jnp.int32),
            pltpu.VMEM(weight.shape, weight.dtype),
            pltpu.VMEM(momentum.shape[1:], momentum.dtype),
            pltpu.VMEM(gradient.shape[1:], gradient.dtype),
            pltpu.VMEM(basis.shape, basis.dtype),
            pltpu.VMEM((kept_count, 2 * tiles), indices.dtype),
            pltpu.VMEM((cols, cols), jnp.int32),
            dma((5,)),
            dma((number,)),
            dma((2, number)),
            dma((number,)),
            dma((number,)),
            dma((4,)),
            dma((3,)),
            dma((CHUNKS,)),
            dma((CHUNKS,)),
            dma((4,)),
            dma((4,)),
        ],
        compiler_params=pltpu.CompilerParams(
            collective_id=0, has_side_effects=True, vmem_limit_bytes=53 * 1024 * 1024
        ),
    )(
        hidden,
        weight,
        momentum,
        gradient,
        listed,
        basis,
    )
    return keys, update, new_momentum


finest_numeric_accuracy = lax.Precision.HIGHEST


def dct_table(length):
    wave_number = jnp.arange(length, dtype=jnp.float32)[:, None]
    position = jnp.arange(length, dtype=jnp.float32)[None, :]
    dct_rows = jnp.cos(jnp.pi * (2.0 * position + 1.0) * wave_number / (2.0 * length)) * jnp.sqrt(
        2.0 / length
    )
    return jnp.where(wave_number == 0.0, dct_rows * jnp.sqrt(0.5), dct_rows)


def make_pair(dct_rows):
    empty_square_tile = jnp.zeros_like(dct_rows)
    upper_half = jnp.concatenate([dct_rows, empty_square_tile], axis=1)
    lower_half = jnp.concatenate([empty_square_tile, dct_rows], axis=1)
    return jnp.concatenate([upper_half, lower_half], axis=0)


def to_spectrum(tile_data, row_basis_operator, paired_cosine_matrix):
    partial_transform = jnp.einsum(
        "ka,tab->tkb", row_basis_operator, tile_data, precision=finest_numeric_accuracy
    )
    return jnp.einsum(
        "tkb,cb->tkc", partial_transform, paired_cosine_matrix, precision=finest_numeric_accuracy
    )


def from_spectrum(tile_frequency_coefficients, row_basis_operator, paired_cosine_matrix):
    partial_transform = jnp.einsum(
        "yh,kyi->khi",
        row_basis_operator,
        tile_frequency_coefficients,
        precision=finest_numeric_accuracy,
    )
    return jnp.einsum(
        "pln,ns->pls", partial_transform, paired_cosine_matrix, precision=finest_numeric_accuracy
    )


def plain(hidden, weight, momentum, gradient, indices, counts):
    tiles_dev, block_side, tile_cols = weight.shape
    kept_count = indices.shape[2]
    replicas = lax.axis_size("rep")
    group_size = lax.axis_size("fsdp")
    all_tiles = tiles_dev * group_size
    width = hidden.shape[1]
    dct_rows = dct_table(block_side)
    paired_cosine_matrix = make_pair(dct_rows)
    moment = decay_rate * momentum[0] + gradient[0].astype(jnp.float32)
    tile_frequency_coefficients = to_spectrum(moment, dct_rows, paired_cosine_matrix)
    span_ids = jnp.arange(2 * tiles_dev, dtype=jnp.int32)[:, None]
    places = (
        span_ids // 2 * (block_side * tile_cols)
        + indices[0] // block_side * tile_cols
        + span_ids % 2 * block_side
        + indices[0] % block_side
    )
    picked = tile_frequency_coefficients.reshape(-1)[places]
    is_live = jnp.arange(kept_count, dtype=jnp.int32)[None, :] < counts[0][:, None]
    kept_values = jnp.where(is_live, picked, jnp.zeros_like(picked))
    flat_size = tiles_dev * block_side * tile_cols
    own_spectra = (
        jnp.zeros((flat_size,), jnp.float32).at[places.reshape(-1)].add(kept_values.reshape(-1))
    )
    own_spectra = own_spectra.reshape(tiles_dev, block_side, tile_cols)
    new_momentum = (moment - from_spectrum(own_spectra, dct_rows, paired_cosine_matrix))[None]
    all_places, all_values = (
        lax.all_gather(places[None], "rep", axis=0, tiled=True),
        lax.all_gather(kept_values[None], "rep", axis=0, tiled=True),
    )
    shared = (
        jnp.zeros((flat_size,), jnp.float32).at[all_places.reshape(-1)].add(all_values.reshape(-1))
    )
    shared = shared.reshape(tiles_dev, block_side, tile_cols) / replicas
    energy = jnp.sum((shared * shared).reshape(tiles_dev, block_side, 2, block_side), axis=(1, 3))
    span_scale = jnp.sqrt(energy / (block_side * block_side) + tiny_eps)
    span_scale = jnp.repeat(span_scale, block_side, axis=1)[:, None, :]
    rows_rep = block_side // replicas
    row_first = lax.axis_index("rep") * rows_rep
    raw_descent_direction = from_spectrum(shared, dct_rows, paired_cosine_matrix)
    update = jnp.tanh(raw_descent_direction / span_scale).astype(jnp.bfloat16)
    revised_parameters = (
        weight.astype(jnp.float32) - step_size * update.astype(jnp.float32)
    ).astype(jnp.bfloat16)
    assembled = lax.all_gather(revised_parameters, "fsdp", axis=0, tiled=True)
    out_update = lax.dynamic_slice_in_dim(update, row_first, rows_rep, 1)
    out_blocks = all_tiles // (width // block_side)
    matrix = assembled.reshape(out_blocks, width // block_side, block_side, tile_cols).transpose(
        1, 2, 0, 3
    )
    matrix = matrix.reshape(width, out_blocks * tile_cols)
    key_states = jnp.dot(hidden, matrix, preferred_element_type=jnp.float32).astype(jnp.bfloat16)
    return (key_states, out_update, new_momentum)


def solution(mesh):
    in_specs = (
        P(("rep", "fsdp"), None),
        P("fsdp", None, None),
        P("rep", "fsdp", None, None),
        P("rep", "fsdp", None, None),
        P("rep", "fsdp", None),
        P("rep", "fsdp"),
    )
    out_specs = (P(("rep", "fsdp"), None), P("fsdp", "rep", None), P("rep", "fsdp", None, None))
    small = mesh.shape["rep"] == 2 and mesh.shape["fsdp"] == 16
    shards = fused if small else plain
    return jax.shard_map(shards, mesh=mesh, in_specs=in_specs, out_specs=out_specs, check_vma=False)
```
